32 devices in a mesh: dp: 8 (over y, x, core), fsdp: 4 (over z).
Axes of the slice: x: 2, y: 2, z: 4, core: 2. Of those that a mesh axis runs over, the one named last changes fastest.
Arguments:
- queries: bfloat16 [4096, 1536], P(('dp', 'fsdp')), may hold values from -6 to 6
- grad_out: bfloat16 [4096, 1536], P(('dp', 'fsdp')), may hold values from -6 to 6
- text_cache: bfloat16 [256, 4096], P('dp', 'fsdp'), may hold values from -6 to 6
- w_kv: bfloat16 [4096, 3072], P('fsdp'), may hold values from -0.09375 to 0.09375
- image_counts: int32 [32, 2], P(('dp', 'fsdp')), may hold values from 1 to 96, 128 in all within a row
- caption_lens: int32 [8, 8], P('dp'), may hold values from 1 to 32, as said below
- caption_owner: int32 [8, 8], P('dp'), may hold values from 0 to 7
- caption_offset: int32 [8, 8], P('dp'), may hold values from 0 to 31, as said below
Outputs:
- grad_queries: bfloat16 [4096, 1536], P(('dp', 'fsdp'))
- grad_kv: bfloat16 [8, 4096, 3072], P('dp', 'fsdp')
The draws below stay inside these ranges and needn't reach their ends.
Inputs may be any that keep to these rules, and one draw needn't show every extreme that they name: caption_offset + caption_lens <= 32 for every caption. `caption_lens`: some caption has exactly 32 tokens and some caption has exactly one.
All inputs are finite; a program needn't handle non-finite values.
Results may differ from the reference program's by a relative error of at most 0.023.
Values may be sent and summed in bfloat16 or wider, within the bound.
No kernel may reach another device: no remote copies, remote signals or barrier semaphores. Data moves between devices by JAX's collectives and lax.ppermute only.
A program may use at most 64 MiB of HBM per device.

```python
import math
import jax
import jax.numpy as jnp
import numpy as np
from jax import lax

TEXT_D = 4096
HEADS = 12
HEAD = 128
LMAX = 32
SAMPLES = 2
TOK_DEV = 128
CR = 32
HD = 1536
TXT_DEV = 64
GROUP_SAMPLES = 8
GROUP_SLOTS = 256
CACHE_ROWS = 256
TOKENS = 4096
N_DP = 8
N_FSDP = 4
DEVICES = 32


def caption_pair(key):
    total = N_DP * GROUP_SAMPLES
    lengths = jax.random.randint(jax.random.fold_in(key, 11), (total,), 1, LMAX + 1)
    marked = jax.random.randint(jax.random.fold_in(key, 12), (), 0, total)
    second = (marked + 1) % total
    lengths = lengths.at[marked].set(LMAX).at[second].set(1)
    spread = jax.random.randint(jax.random.fold_in(key, 13), (total,), 0, CR)
    offsets = spread % (CR - lengths + 1)
    offsets = offsets.at[marked].set(0).at[second].set(CR - 1)
    return (lengths.reshape(N_DP, GROUP_SAMPLES).astype(jnp.int32), offsets.reshape(N_DP, GROUP_SAMPLES).astype(jnp.int32))


def draw_caption_lens(key, part):
    return caption_pair(key)[0]


def draw_caption_offset(key, part):
    return caption_pair(key)[1]


def touch_ends(entries, key, smallest, high):
    dims = entries.shape
    place = [jax.random.randint(jax.random.fold_in(key, axis), (), 0, dims[axis]) for axis in range(len(dims))]
    entries = entries.at[tuple(place)].set(smallest)
    longest = dims.index(max(dims))
    place[longest] = (place[longest] + 1) % dims[longest]
    return entries.at[tuple(place)].set(high)


def shard_levels(stream_key, extent, cuts, low, largest):
    loudness, own = 1.0, jax.random.fold_in(stream_key, 6)
    for axis_at, parts in cuts:
        heights = jnp.exp(jax.random.uniform(jax.random.fold_in(own, axis_at), (parts,), jnp.float32, low / len(cuts), largest / len(cuts)))
        loudness = loudness * jnp.repeat(heights, extent[axis_at] // parts).reshape([-1 if axis == axis_at else 1 for axis in range(len(extent))])
    return loudness


def split_up(amount, total, most, slope):
    loads = [(1 << 20) // math.isqrt(grade ** slope) + 1 for grade in range(2, amount + 1)]
    rest, given = total - most - (amount - 1), [1] * (amount - 1)
    while rest > 0:
        movable = [i for i in range(amount - 1) if given[i] < most]
        mass, budget = sum([loads[i] for i in movable]), rest
        for i in movable:
            more = min(most - given[i], max(1, budget * loads[i] // mass), rest)
            given[i] = given[i] + more
            rest = rest - more
    return np.array([most] + given)


def ragged_sizes(own_key, amount, total, bound, slope):
    if amount == 2:
        one = jax.random.randint(own_key, (), max(1, total - bound), min(bound, total - 1) + 1)
        return jnp.stack([one, total - one])
    tallies = jnp.asarray(split_up(amount, total, bound, slope), jnp.int32)
    pairs = (amount - 1) // 2
    donor, taker = tallies[1:1 + 2 * pairs:2], tallies[2:2 + 2 * pairs:2]
    margin = jnp.minimum(donor - 1, bound - taker)
    passed = jax.random.randint(jax.random.fold_in(own_key, 1), (pairs,), 0, 1 << 20) % (margin + 1)
    tallies = tallies.at[1:1 + 2 * pairs:2].set(donor - passed).at[2:2 + 2 * pairs:2].set(taker + passed)
    return tallies[jax.random.permutation(jax.random.fold_in(own_key, 2), amount)]


def gaussian(rng, shape, deviation, bound, cuts=(), kind=jnp.bfloat16):
    array = jax.random.normal(rng, shape, jnp.float32) * deviation
    if len(cuts) > 0:
        array = shard_levels(rng, shape, cuts, -0.22, 0.18) * array
    return jnp.clip(array, min=-bound, max=bound).astype(kind)


def setup_inputs(seed: int = 0) -> dict:
    streams_of = jax.random.split(jax.random.key(seed), 9)
    queries = gaussian(streams_of[0], (TOKENS, HD), 1.0, 6.0, ((0, 32),))
    grad_out = gaussian(streams_of[1], (TOKENS, HD), 1.0, 6.0, ((0, 32),))
    text_cache = gaussian(streams_of[2], (CACHE_ROWS, TEXT_D), 1.0, 6.0, ((0, 8), (1, 4)))
    w_kv = gaussian(streams_of[3], (TEXT_D, 2 * HD), TEXT_D ** -0.5, 0.09375, ((0, 4),))
    image_counts = jax.vmap(lambda own: ragged_sizes(own, SAMPLES, TOK_DEV, TOK_DEV * 3 // 4, 0))(jax.random.split(streams_of[4], DEVICES)).reshape((DEVICES, SAMPLES)).astype(jnp.int32)
    caption_lens = draw_caption_lens(jax.random.fold_in(streams_of[8], 71), 0)
    caption_owner = touch_ends(jax.random.randint(streams_of[6], (N_DP, GROUP_SAMPLES), 0, N_DP), jax.random.fold_in(streams_of[6], 1), 0, N_DP - 1).astype(jnp.int32)
    caption_offset = draw_caption_offset(jax.random.fold_in(streams_of[8], 71), 0)
    return dict(queries=queries, grad_out=grad_out, text_cache=text_cache, w_kv=w_kv, image_counts=image_counts, caption_lens=caption_lens, caption_owner=caption_owner, caption_offset=caption_offset)


def reference(queries, grad_out, text_cache, w_kv, image_counts, caption_lens, caption_owner, caption_offset):
    attn_scale = HEAD ** -0.5

    def group_grads(operands):
        query_group, cotangent_group, counts_group, lengths, owners, offsets = operands
        slot_steps = jnp.arange(LMAX, dtype=jnp.int32)
        wanted = (owners[:, None] * CR + offsets[:, None] + slot_steps[None, :]).reshape(-1)
        wanted = jnp.clip(wanted, 0, CACHE_ROWS - 1).astype(jnp.int32)
        live_slot = (slot_steps[None, :] < lengths[:, None]).reshape(-1)
        fetched = jnp.where(live_slot[:, None], text_cache[wanted], jnp.zeros((), jnp.bfloat16))
        blocks = fetched.reshape(GROUP_SLOTS, N_FSDP, TEXT_D // N_FSDP).astype(jnp.float32)
        weight_blocks = w_kv.reshape(N_FSDP, TEXT_D // N_FSDP, 2 * HD).astype(jnp.float32)
        partial_value = jnp.einsum("snc,nce->nse", blocks, weight_blocks, precision=lax.Precision.HIGHEST)
        rounded = lax.optimization_barrier(partial_value.astype(jnp.bfloat16)).astype(jnp.float32)
        keys_values = jnp.sum(rounded, axis=0).astype(jnp.bfloat16)
        query_heads = query_group.reshape(N_FSDP, TOK_DEV, HEADS, HEAD).astype(jnp.float32)
        cotangent_heads = cotangent_group.reshape(N_FSDP, TOK_DEV, HEADS, HEAD).astype(jnp.float32)
        key_heads = keys_values[:, :HD].reshape(N_FSDP, TXT_DEV, HEADS, HEAD).astype(jnp.float32)
        value_heads = keys_values[:, HD:].reshape(N_FSDP, TXT_DEV, HEADS, HEAD).astype(jnp.float32)
        positions = jnp.arange(TOK_DEV, dtype=jnp.int32)
        sample_ends = jnp.cumsum(counts_group, axis=1)
        token_sample = jnp.sum((positions[None, :, None] >= sample_ends[:, None, :SAMPLES - 1]).astype(jnp.int32), axis=2)
        slot_sample = jnp.arange(TXT_DEV, dtype=jnp.int32) // LMAX
        slot_open = live_slot.reshape(N_FSDP, TXT_DEV)
        allowed = (token_sample[:, :, None] == slot_sample[None, None, :]) & slot_open[:, None, :]
        scores = jnp.einsum("nthe,nshe->nhts", query_heads, key_heads) * attn_scale
        scores = jnp.where(allowed[:, None], scores, jnp.float32(-1e30))
        row_top = jnp.max(scores, axis=-1, keepdims=True)
        expon = jnp.exp(scores - row_top)
        probabilities = expon / jnp.sum(expon, axis=-1, keepdims=True)
        prob_grads = jnp.einsum("nthe,nshe->nhts", cotangent_heads, value_heads)
        centre = jnp.sum(probabilities * prob_grads, axis=-1, keepdims=True)
        score_grads = lax.optimization_barrier((probabilities * (prob_grads - centre)).astype(jnp.bfloat16)).astype(jnp.float32)
        probs_rounded = lax.optimization_barrier(probabilities.astype(jnp.bfloat16)).astype(jnp.float32)
        grad_query = (jnp.einsum("nhts,nshe->nthe", score_grads, key_heads) * attn_scale).astype(jnp.bfloat16)
        grad_key = jnp.einsum("nhts,nthe->nshe", score_grads, query_heads) * attn_scale
        grad_value = jnp.einsum("nhts,nthe->nshe", probs_rounded, cotangent_heads)
        grad_slots = jnp.concatenate([grad_key.reshape(GROUP_SLOTS, HD), grad_value.reshape(GROUP_SLOTS, HD)], axis=1).astype(jnp.bfloat16)
        grad_weight = jnp.dot(fetched.T, grad_slots, preferred_element_type=jnp.float32).astype(jnp.bfloat16)
        return grad_query.reshape(N_FSDP * TOK_DEV, HD), grad_weight

    operands = (queries.reshape(N_DP, N_FSDP * TOK_DEV, HD), grad_out.reshape(N_DP, N_FSDP * TOK_DEV, HD), image_counts.reshape(N_DP, N_FSDP, SAMPLES), caption_lens, caption_owner, caption_offset)
    grad_query_all, grad_weight_all = lax.map(group_grads, operands)
    return grad_query_all.reshape(TOKENS, HD), grad_weight_all
```

```python
import functools

import jax
import jax.numpy as jnp
from jax import lax
from jax.experimental import pallas as pl
from jax.experimental.pallas import tpu as pltpu
from jax.sharding import PartitionSpec as P

HEADS = 12
HEAD = 128
LMAX = 32
SAMPLES = 2
VMEM = 48 * 1024 * 1024

F32 = jnp.float32
BF16 = jnp.bfloat16


def power_of_two(n):
    return n & (n - 1) == 0


def kernel_params(**more):
    return pltpu.CompilerParams(vmem_limit_bytes=VMEM, **more)


SMEM_SPEC = pl.BlockSpec(memory_space=pltpu.SMEM)
VMEM_SPEC = pl.BlockSpec(memory_space=pltpu.VMEM)


def scalar_table(image_counts, caption_lens, caption_owner, caption_offset):
    captions = caption_lens.shape[1]
    place = jnp.stack([lax.axis_index("dp"), lax.axis_index("fsdp"), image_counts[0, 0]]).astype(jnp.int32)
    place = jnp.pad(place, (0, captions - place.shape[0]))
    return jnp.concatenate([caption_lens, caption_owner, caption_offset, place[None]], axis=0)


def peer(index, k, paired):
    return index ^ k if paired else k


def first_of_class(offset, residue, groups):
    return lax.div(offset - residue + groups - 1, jnp.int32(groups))


def spread_rows(values, rows_each, shape):
    rows = lax.broadcasted_iota(jnp.int32, shape, 0)
    result = jnp.zeros(shape, jnp.int32)
    for g, value in enumerate(values):
        result = jnp.where((rows >= g * rows_each) & (rows < (g + 1) * rows_each), value + rows - g * rows_each, result)
    return result


def project_kernel(groups, paired, table, cache, weight, *outs):
    depth = cache.shape[0]
    each = depth // groups
    member = table[3, 1]
    rows = lax.broadcasted_iota(jnp.int32, (depth, depth), 0)
    columns = lax.broadcasted_iota(jnp.int32, (depth, depth), 1)
    wanted = jnp.zeros((depth, depth), jnp.int32)
    for k in range(groups):
        wanted = jnp.where(rows // each == k, groups * (rows - k * each) + peer(member, k, paired), wanted)
    order = (wanted == columns).astype(BF16)
    sorted_rows = jnp.dot(order, cache[...], preferred_element_type=F32).astype(BF16)
    product = jnp.dot(sorted_rows, weight[...], preferred_element_type=F32)
    for k in range(groups):
        outs[k][...] = product[k * each : (k + 1) * each].astype(BF16)


def project(groups, paired, table, text_cache, w_kv):
    depth, features = text_cache.shape
    width = w_kv.shape[1]
    block = 512
    each = depth // groups
    return pl.pallas_call(
        functools.partial(project_kernel, groups, paired),
        grid=(width // block,),
        in_specs=[
            SMEM_SPEC,
            pl.BlockSpec((depth, features), lambda n: (0, 0)),
            pl.BlockSpec((features, block), lambda n: (0, n)),
        ],
        out_specs=[pl.BlockSpec((each, block), lambda n: (0, n))] * groups,
        out_shape=[jax.ShapeDtypeStruct((each, width), BF16)] * groups,
        compiler_params=kernel_params(),
        name="project",
    )(table, text_cache, w_kv)


def select_kernel(groups, each, paired, dp_paired, table, *refs):
    pieces, outs = refs[:-groups], refs[-groups:]
    held = jnp.concatenate([piece[...] for piece in pieces], axis=0) if len(pieces) > 1 else pieces[0][...]
    total = held.shape[0]
    index, member = table[3, 0], table[3, 1]
    wanted_rows = groups * SAMPLES * each
    starts, firsts = [], []
    for k in range(groups):
        for s in range(SAMPLES):
            caption = peer(member, k, paired) * SAMPLES + s
            first = first_of_class(table[2, caption], member, groups)
            owner = table[1, caption]
            firsts.append(first)
            starts.append((owner ^ index if dp_paired else owner) * each + first)
    shape = (wanted_rows, total)
    target = spread_rows(starts, each, shape)
    inside = spread_rows(firsts, each, shape) < each
    chosen = ((target == lax.broadcasted_iota(jnp.int32, shape, 1)) & inside).astype(BF16)
    rows = jnp.dot(chosen, held, preferred_element_type=F32).astype(BF16)
    size = SAMPLES * each
    for k in range(groups):
        outs[k][...] = rows[k * size : (k + 1) * size]


def select_rows(groups, each, paired, dp_paired, table, pieces):
    width = pieces[0].shape[1]
    return pl.pallas_call(
        functools.partial(select_kernel, groups, each, paired, dp_paired),
        in_specs=[SMEM_SPEC] + [VMEM_SPEC] * len(pieces),
        out_specs=[VMEM_SPEC] * groups,
        out_shape=[jax.ShapeDtypeStruct((SAMPLES * each, width), BF16)] * groups,
        compiler_params=kernel_params(),
        name="select_rows",
    )(table, *pieces)


def attention_kernel(groups, each, paired, table, queries, cotangent, *refs):
    pieces, (grad_query, grad_slots) = refs[:groups], refs[groups:]
    tokens, width = queries.shape
    slots = groups * SAMPLES * each
    scale = HEAD ** (-0.5)
    member = table[3, 1]
    split = table[3, 2]
    shape = (slots, tokens)
    rows = lax.broadcasted_iota(jnp.int32, shape, 0)
    position = jnp.zeros(shape, jnp.int32)
    length = jnp.zeros(shape, jnp.int32)
    sample = jnp.zeros(shape, jnp.int32)
    for c in range(groups):
        residue = peer(member, c, paired)
        for s in range(SAMPLES):
            caption = member * SAMPLES + s
            run = (c * SAMPLES + s) * each
            here = (rows >= run) & (rows < run + each)
            first = first_of_class(table[2, caption], residue, groups)
            position = jnp.where(here, groups * (first + rows - run) + residue - table[2, caption], position)
            length = jnp.where(here, table[0, caption], length)
            sample = jnp.where(here, s, sample)
    token_sample = (lax.broadcasted_iota(jnp.int32, shape, 1) >= split).astype(jnp.int32)
    allowed = (position < length) & (sample == token_sample)
    last = (((1,), (1,)), ((), ()))
    first_dims = (((0,), (0,)), ((), ()))
    for h in range(width // HEAD):
        at = slice(h * HEAD, (h + 1) * HEAD)
        values_at = slice(width + h * HEAD, width + (h + 1) * HEAD)
        q, g = queries[:, at], cotangent[:, at]
        k = jnp.concatenate([piece[:, at] for piece in pieces], axis=0)
        v = jnp.concatenate([piece[:, values_at] for piece in pieces], axis=0)
        scores = lax.dot_general(k, q, last, preferred_element_type=F32) * scale
        scores = jnp.where(allowed, scores, F32(-1e30))
        expon = jnp.exp(scores - jnp.max(scores, axis=0, keepdims=True))
        probs = expon / jnp.sum(expon, axis=0, keepdims=True)
        prob_grads = lax.dot_general(v, g, last, preferred_element_type=F32)
        centre = jnp.sum(probs * prob_grads, axis=0, keepdims=True)
        score_grads = (probs * (prob_grads - centre)).astype(BF16)
        grad_query[:, at] = (lax.dot_general(score_grads, k, first_dims, preferred_element_type=F32) * scale).astype(BF16)
        grad_slots[:, at] = (jnp.dot(score_grads, q, preferred_element_type=F32) * scale).astype(BF16)
        grad_slots[:, values_at] = jnp.dot(probs.astype(BF16), g, preferred_element_type=F32).astype(BF16)


def attention(groups, each, paired, table, queries, grad_out, pieces):
    tokens, width = queries.shape
    slots = groups * SAMPLES * each
    return pl.pallas_call(
        functools.partial(attention_kernel, groups, each, paired),
        in_specs=[SMEM_SPEC] + [VMEM_SPEC] * (2 + groups),
        out_specs=[VMEM_SPEC] * 2,
        out_shape=[
            jax.ShapeDtypeStruct((tokens, width), BF16),
            jax.ShapeDtypeStruct((slots, 2 * width), BF16),
        ],
        compiler_params=kernel_params(),
        name="attention_backward",
    )(table, queries, grad_out, *pieces)


def weight_kernel(groups, each, depth, paired, dp_paired, order, n_text, n_grads, table, *refs):
    texts, grads = refs[:n_text], refs[n_text : n_text + n_grads]
    out, chosen_text = refs[n_text + n_grads :]
    index, member = table[3, 0], table[3, 1]

    @pl.when(pl.program_id(0) == 0)
    def _():
        held = jnp.concatenate([text[...] for text in texts], axis=0) if n_text > 1 else texts[0][...]
        bases, limits = [], []
        for k in range(groups):
            device = peer(member, k, paired)
            for c in range(groups):
                residue = peer(device, c, paired)
                for s in range(SAMPLES):
                    caption = device * SAMPLES + s
                    first = first_of_class(table[2, caption], residue, groups)
                    owner = table[1, caption]
                    base = (owner ^ index if dp_paired else owner) * depth
                    bases.append((base + groups * first + residue, base + table[2, caption] + table[0, caption]))
        shape = (held.shape[0], groups * groups * SAMPLES * each)
        columns = lax.broadcasted_iota(jnp.int32, shape, 1)
        runs, place = columns // each, columns % each
        target = jnp.zeros(shape, jnp.int32)
        limit = jnp.zeros(shape, jnp.int32)
        for g, (base, end) in enumerate(bases):
            target = jnp.where(runs == g, base, target)
            limit = jnp.where(runs == g, end, limit)
        target = target + groups * place
        chosen = ((target == lax.broadcasted_iota(jnp.int32, shape, 0)) & (target < limit)).astype(BF16)
        first_dims = (((0,), (0,)), ((), ()))
        chosen_text[...] = lax.dot_general(held, chosen, first_dims, preferred_element_type=F32).astype(BF16)

    if order == "chain":
        near, inner1, inner2, outer1, outer2, own = [g[...] for g in grads]
        inner = (member == 1) | (member == 2)
        pieces = [own, near, jnp.where(inner, inner2, outer1), jnp.where(inner, inner1, outer2)]
        every = jnp.concatenate(pieces, axis=0)
    else:
        every = grads[0][...]
    out[...] = jnp.dot(chosen_text[...], every, preferred_element_type=F32).astype(BF16)


def weight_grad(groups, each, depth, paired, dp_paired, order, table, texts, grads):
    features = texts[0].shape[1]
    slots, width = grads[0].shape
    total = groups * groups * SAMPLES * each
    block = 512
    return pl.pallas_call(
        functools.partial(weight_kernel, groups, each, depth, paired, dp_paired, order, len(texts), len(grads)),
        grid=(width // block,),
        in_specs=[SMEM_SPEC]
        + [pl.BlockSpec(t.shape, lambda n: (0, 0)) for t in texts]
        + [pl.BlockSpec((g.shape[0], block), lambda n: (0, n)) for g in grads],
        out_specs=pl.BlockSpec((features, block), lambda n: (0, n)),
        out_shape=jax.ShapeDtypeStruct((features, width), BF16),
        scratch_shapes=[pltpu.VMEM((features, total), BF16)],
        compiler_params=kernel_params(),
        name="weight_gradient",
    )(table, *texts, *grads)


def swap(x, axis, k):
    return lax.ppermute(x, axis, [(i, i ^ k) for i in range(lax.axis_size(axis))])


def gather_dp(x, paired):
    if not paired:
        return [lax.all_gather(x, "dp", axis=0, tiled=True)]
    near = {0: x}
    for k in range(2, lax.axis_size("dp"), 2):
        near[k] = swap(x, "dp", k)
    for k in list(near):
        near[k + 1] = swap(near[k], "dp", 1)
    return [near[k] for k in sorted(near)]


def exchange(pieces, paired):
    if paired:
        return [pieces[0]] + [swap(pieces[k], "fsdp", k) for k in range(1, len(pieces))]
    came = lax.all_to_all(jnp.stack(pieces), "fsdp", 0, 0, tiled=True)
    return [came[k] for k in range(len(pieces))]


def gather_line(x):
    near_pairs = [(0, 1), (1, 0), (2, 3), (3, 2)]
    middle_pairs = [(1, 2), (2, 1)]
    outward = [(1, 0), (2, 3)]
    near = lax.ppermute(x, "fsdp", near_pairs)
    inner1 = lax.ppermute(x, "fsdp", middle_pairs)
    inner2 = lax.ppermute(near, "fsdp", middle_pairs)
    outer1 = lax.ppermute(inner1, "fsdp", outward)
    outer2 = lax.ppermute(inner2, "fsdp", outward)
    return [near, inner1, inner2, outer1, outer2, x]


def shards(
    queries, grad_out, text_cache, w_kv, image_counts, caption_lens, caption_owner, caption_offset
):
    groups = lax.axis_size("fsdp")
    line = groups == 4
    paired = line
    dp_paired = power_of_two(lax.axis_size("dp")) and lax.axis_size("dp") <= 8
    depth = text_cache.shape[0]
    each = depth // groups
    table = scalar_table(image_counts, caption_lens, caption_owner, caption_offset)

    partials = project(groups, paired, table, text_cache, w_kv)
    came = exchange(partials, paired)
    rows = sum(piece.astype(F32) for piece in came).astype(BF16)
    class_rows = gather_dp(rows, dp_paired)
    outgoing = select_rows(groups, each, paired, dp_paired, table, class_rows)
    keys_values = exchange(outgoing, paired)
    grad_query, grad_slots = attention(groups, each, paired, table, queries, grad_out, keys_values)
    grad_slots, late_cache = lax.optimization_barrier((grad_slots, text_cache))
    texts = gather_dp(late_cache, dp_paired)
    if line:
        grads = gather_line(grad_slots)
    else:
        grads = [lax.all_gather(grad_slots, "fsdp", axis=0, tiled=True)]
    grad_weight = weight_grad(
        groups, each, depth, paired, dp_paired, "chain" if line else "whole", table, texts, grads
    )
    return grad_query, grad_weight[None]


def solution(mesh):
    in_specs = (
        P(("dp", "fsdp"), None),
        P(("dp", "fsdp"), None),
        P("dp", "fsdp"),
        P("fsdp", None),
        P(("dp", "fsdp"), None),
        P("dp", None),
        P("dp", None),
        P("dp", None),
    )
    out_specs = (P(("dp", "fsdp"), None), P("dp", "fsdp", None))
    return jax.shard_map(shards, mesh=mesh, in_specs=in_specs, out_specs=out_specs, check_vma=False)
```

```python
import functools

import jax
import jax.numpy as jnp
from jax import lax
from jax.experimental import pallas as pl
from jax.experimental.pallas import tpu as pltpu
from jax.sharding import PartitionSpec as P

HEADS = 12
HEAD = 128
LMAX = 32
SAMPLES = 2
VMEM = 48 * 1024 * 1024

F32 = jnp.float32
BF16 = jnp.bfloat16


def power_of_two(n):
    return n & (n - 1) == 0


def kernel_params(**more):
    return pltpu.CompilerParams(vmem_limit_bytes=VMEM, **more)


SMEM_SPEC = pl.BlockSpec(memory_space=pltpu.SMEM)
VMEM_SPEC = pl.BlockSpec(memory_space=pltpu.VMEM)
ANY_SPEC = pl.BlockSpec(memory_space=pl.ANY)
HBM_SPEC = pl.BlockSpec(memory_space=pltpu.HBM)


def scalar_table(image_counts, caption_lens, caption_owner, caption_offset):
    captions = caption_lens.shape[1]
    place = jnp.stack([lax.axis_index("dp"), lax.axis_index("fsdp"), image_counts[0, 0]]).astype(jnp.int32)
    place = jnp.pad(place, (0, captions - place.shape[0]))
    return jnp.concatenate([caption_lens, caption_owner, caption_offset, place[None]], axis=0)


def peer(index, k, paired):
    return index ^ k if paired else k


def first_of_class(offset, residue, groups):
    return lax.div(offset - residue + groups - 1, jnp.int32(groups))


def spread_rows(values, rows_each, shape):
    rows = lax.broadcasted_iota(jnp.int32, shape, 0)
    result = jnp.zeros(shape, jnp.int32)
    for g, value in enumerate(values):
        result = jnp.where((rows >= g * rows_each) & (rows < (g + 1) * rows_each), value + rows - g * rows_each, result)
    return result


def project_kernel(groups, paired, chunks, cache, weight, *refs):
    outs = refs[:groups]
    held_cache, held_weight, cache_sem, weight_sem = refs[groups:]
    depth = cache.shape[0]
    each = depth // groups
    rows = weight.shape[0] // chunks
    cache_copy = pltpu.make_async_copy(cache, held_cache, cache_sem)
    cache_copy.start()
    copies = [
        pltpu.make_async_copy(weight.at[pl.ds(i * rows, rows)], held_weight.at[pl.ds(i * rows, rows)], weight_sem.at[i])
        for i in range(chunks)
    ]
    for copy in copies:
        copy.start()
    member = lax.axis_index("fsdp")
    row = lax.broadcasted_iota(jnp.int32, (depth, depth), 0)
    column = lax.broadcasted_iota(jnp.int32, (depth, depth), 1)
    wanted = jnp.zeros((depth, depth), jnp.int32)
    for k in range(groups):
        wanted = jnp.where(row // each == k, groups * (row - k * each) + peer(member, k, paired), wanted)
    order = (wanted == column).astype(BF16)
    cache_copy.wait()
    sorted_rows = jnp.dot(order, held_cache[...], preferred_element_type=F32).astype(BF16)
    product = None
    for i, copy in enumerate(copies):
        copy.wait()
        at = slice(i * rows, (i + 1) * rows)
        part = jnp.dot(sorted_rows[:, at], held_weight[at], preferred_element_type=F32)
        product = part if product is None else product + part
    for k in range(groups):
        outs[k][...] = product[k * each : (k + 1) * each].astype(BF16)


def project(groups, paired, text_cache, w_kv):
    depth, features = text_cache.shape
    width = w_kv.shape[1]
    chunks = features // 128
    each = depth // groups
    return pl.pallas_call(
        functools.partial(project_kernel, groups, paired, chunks),
        in_specs=[HBM_SPEC, HBM_SPEC],
        out_specs=[VMEM_SPEC] * groups,
        out_shape=[jax.ShapeDtypeStruct((each, width), BF16)] * groups,
        scratch_shapes=[
            pltpu.VMEM((depth, features), BF16),
            pltpu.VMEM((features, width), BF16),
            pltpu.SemaphoreType.DMA,
            pltpu.SemaphoreType.DMA((chunks,)),
        ],
        compiler_params=kernel_params(),
        name="project",
    )(text_cache, w_kv)


def select_kernel(groups, each, paired, dp_paired, table, *refs):
    pieces, outs = refs[:-groups], refs[-groups:]
    held = jnp.concatenate([piece[...] for piece in pieces], axis=0) if len(pieces) > 1 else pieces[0][...]
    total = held.shape[0]
    index, member = table[3, 0], table[3, 1]
    wanted_rows = groups * SAMPLES * each
    starts, firsts = [], []
    for k in range(groups):
        for s in range(SAMPLES):
            caption = peer(member, k, paired) * SAMPLES + s
            first = first_of_class(table[2, caption], member, groups)
            owner = table[1, caption]
            firsts.append(first)
            starts.append((owner ^ index if dp_paired else owner) * each + first)
    shape = (wanted_rows, total)
    target = spread_rows(starts, each, shape)
    inside = spread_rows(firsts, each, shape) < each
    chosen = ((target == lax.broadcasted_iota(jnp.int32, shape, 1)) & inside).astype(BF16)
    rows = jnp.dot(chosen, held, preferred_element_type=F32).astype(BF16)
    size = SAMPLES * each
    for k in range(groups):
        outs[k][...] = rows[k * size : (k + 1) * size]


def select_rows(groups, each, paired, dp_paired, table, pieces):
    width = pieces[0].shape[1]
    return pl.pallas_call(
        functools.partial(select_kernel, groups, each, paired, dp_paired),
        in_specs=[SMEM_SPEC] + [VMEM_SPEC] * len(pieces),
        out_specs=[VMEM_SPEC] * groups,
        out_shape=[jax.ShapeDtypeStruct((SAMPLES * each, width), BF16)] * groups,
        compiler_params=kernel_params(),
        name="select_rows",
    )(table, *pieces)


LAST = (((1,), (1,)), ((), ()))
FIRST = (((0,), (0,)), ((), ()))


def value_grad_kernel(groups, each, paired, table, queries, cotangent, *refs):
    pieces, (probs, probs_rounded, grad_values, scores) = refs[:groups], refs[groups:]
    tokens, width = queries.shape
    slots = groups * SAMPLES * each
    heads = width // HEAD
    member = table[3, 1]
    split = table[3, 2]
    shape = (slots, tokens)
    rows = lax.broadcasted_iota(jnp.int32, shape, 0)
    position = jnp.zeros(shape, jnp.int32)
    length = jnp.zeros(shape, jnp.int32)
    sample = jnp.zeros(shape, jnp.int32)
    for c in range(groups):
        residue = peer(member, c, paired)
        for s in range(SAMPLES):
            caption = member * SAMPLES + s
            run = (c * SAMPLES + s) * each
            here = (rows >= run) & (rows < run + each)
            first = first_of_class(table[2, caption], residue, groups)
            position = jnp.where(here, groups * (first + rows - run) + residue - table[2, caption], position)
            length = jnp.where(here, table[0, caption], length)
            sample = jnp.where(here, s, sample)
    token_sample = (lax.broadcasted_iota(jnp.int32, shape, 1) >= split).astype(jnp.int32)
    allowed = (position < length) & (sample == token_sample)
    for h in range(heads):
        at = slice(h * HEAD, (h + 1) * HEAD)
        k = jnp.concatenate([piece[:, at] for piece in pieces], axis=0)
        scores[h] = lax.dot_general(k, queries[:, at], LAST, preferred_element_type=F32)
    for h in range(heads):
        masked = jnp.where(allowed, scores[h] * HEAD ** (-0.5), F32(-1e30))
        expon = jnp.exp(masked - jnp.max(masked, axis=0, keepdims=True))
        prob = expon / jnp.sum(expon, axis=0, keepdims=True)
        probs[h] = prob
        probs_rounded[h] = prob.astype(BF16)
    for h in range(heads):
        at = slice(h * HEAD, (h + 1) * HEAD)
        grad_values[:, at] = jnp.dot(probs_rounded[h], cotangent[:, at], preferred_element_type=F32).astype(BF16)


def value_grads(groups, each, paired, table, queries, grad_out, pieces):
    tokens, width = queries.shape
    slots = groups * SAMPLES * each
    heads = width // HEAD
    return pl.pallas_call(
        functools.partial(value_grad_kernel, groups, each, paired),
        in_specs=[SMEM_SPEC] + [VMEM_SPEC] * (2 + groups),
        out_specs=[VMEM_SPEC] * 3,
        out_shape=[
            jax.ShapeDtypeStruct((heads, slots, tokens), F32),
            jax.ShapeDtypeStruct((heads, slots, tokens), BF16),
            jax.ShapeDtypeStruct((slots, width), BF16),
        ],
        scratch_shapes=[pltpu.VMEM((heads, slots, tokens), F32)],
        compiler_params=kernel_params(),
        name="value_gradients",
    )(table, queries, grad_out, *pieces)


def key_grad_kernel(groups, probs, queries, cotangent, grad_values, *refs):
    pieces, (grad_query, grad_keys, grad_both, prob_grads, score_grads) = refs[:groups], refs[groups:]
    width = queries.shape[1]
    heads = width // HEAD
    scale = HEAD ** (-0.5)
    for h in range(heads):
        values_at = slice(width + h * HEAD, width + (h + 1) * HEAD)
        v = jnp.concatenate([piece[:, values_at] for piece in pieces], axis=0)
        prob_grads[h] = lax.dot_general(v, cotangent[:, h * HEAD : (h + 1) * HEAD], LAST, preferred_element_type=F32)
    for h in range(heads):
        prob, prob_grad = probs[h], prob_grads[h]
        centre = jnp.sum(prob * prob_grad, axis=0, keepdims=True)
        score_grads[h] = (prob * (prob_grad - centre)).astype(BF16)
    for h in range(heads):
        at = slice(h * HEAD, (h + 1) * HEAD)
        k = jnp.concatenate([piece[:, at] for piece in pieces], axis=0)
        score_grad = score_grads[h]
        grad_key = (jnp.dot(score_grad, queries[:, at], preferred_element_type=F32) * scale).astype(BF16)
        grad_keys[:, at] = grad_key
        grad_both[:, at] = grad_key
        grad_query[:, at] = (lax.dot_general(score_grad, k, FIRST, preferred_element_type=F32) * scale).astype(BF16)
    grad_both[:, width:] = grad_values[...]


def key_grads(groups, probs, queries, grad_out, grad_values, pieces):
    tokens, width = queries.shape
    heads, slots, _ = probs.shape
    return pl.pallas_call(
        functools.partial(key_grad_kernel, groups),
        in_specs=[VMEM_SPEC] * (4 + groups),
        out_specs=[VMEM_SPEC] * 3,
        out_shape=[
            jax.ShapeDtypeStruct((tokens, width), BF16),
            jax.ShapeDtypeStruct((slots, width), BF16),
            jax.ShapeDtypeStruct((slots, 2 * width), BF16),
        ],
        scratch_shapes=[pltpu.VMEM((heads, slots, tokens), F32), pltpu.VMEM((heads, slots, tokens), BF16)],
        compiler_params=kernel_params(),
        name="key_gradients",
    )(probs, queries, grad_out, grad_values, *pieces)


def text_kernel(groups, each, depth, paired, dp_paired, table, *refs):
    texts, out = refs[:-1], refs[-1]
    index, member = table[3, 0], table[3, 1]
    held = jnp.concatenate([text[...] for text in texts], axis=0) if len(texts) > 1 else texts[0][...]
    shape = (held.shape[0], out.shape[1])
    columns = lax.broadcasted_iota(jnp.int32, shape, 1)
    runs, place = columns // each, columns % each
    target = jnp.zeros(shape, jnp.int32)
    limit = jnp.zeros(shape, jnp.int32)
    run = 0
    for k in range(groups):
        device = peer(member, k, paired)
        for c in range(groups):
            residue = peer(device, c, paired)
            for s in range(SAMPLES):
                caption = device * SAMPLES + s
                offset = table[2, caption]
                owner = table[1, caption]
                base = (owner ^ index if dp_paired else owner) * depth
                here = runs == run
                target = jnp.where(here, base + groups * first_of_class(offset, residue, groups) + residue, target)
                limit = jnp.where(here, base + offset + table[0, caption], limit)
                run += 1
    target = target + groups * place
    chosen = ((target == lax.broadcasted_iota(jnp.int32, shape, 0)) & (target < limit)).astype(BF16)
    out[...] = lax.dot_general(held, chosen, FIRST, preferred_element_type=F32).astype(BF16)


def slot_texts(groups, each, depth, paired, dp_paired, table, texts):
    features = texts[0].shape[1]
    return pl.pallas_call(
        functools.partial(text_kernel, groups, each, depth, paired, dp_paired),
        in_specs=[SMEM_SPEC] + [VMEM_SPEC] * len(texts),
        out_specs=VMEM_SPEC,
        out_shape=jax.ShapeDtypeStruct((features, groups * groups * SAMPLES * each), BF16),
        compiler_params=kernel_params(),
        name="slot_texts",
    )(table, *texts)


def weight_kernel(line, first, block, started, *refs):
    chosen_text, *grads = refs[: -4 if started else -3]
    out, built, sems = refs[-3:]
    part = built.shape[1]
    if line:
        member = lax.axis_index("fsdp")
        is_inner = (member == 1) | (member == 2)
    copies = []
    for i in range(part // block):
        at = slice(i * block, (i + 1) * block)
        if line:
            own, near, second, inner, outer = [g[:, at] for g in grads]
            every = jnp.concatenate([own, near, second, jnp.where(is_inner, inner, outer)], axis=0)
        else:
            every = grads[0][:, at]
        built[:, at] = jnp.dot(chosen_text[...], every, preferred_element_type=F32).astype(BF16)
        copy = pltpu.make_async_copy(
            built.at[:, pl.ds(i * block, block)], out.at[:, pl.ds(first + i * block, block)], sems.at[i]
        )
        copy.start()
        copies.append(copy)
    for copy in copies:
        copy.wait()


def weight_grad(line, chosen_text, grads, width, first, before=None):
    features, slots = chosen_text.shape
    part = grads[0].shape[1]
    block = 256
    started = before is not None
    parts = [pl.BlockSpec((g.shape[0], part), lambda n, at=first // part * (g.shape[1] > part): (0, at)) for g in grads]
    return pl.pallas_call(
        functools.partial(weight_kernel, line, first, block, started),
        grid=(1,),
        in_specs=[pl.BlockSpec((features, slots), lambda n: (0, 0))] + parts + [ANY_SPEC] * started,
        out_specs=ANY_SPEC,
        out_shape=jax.ShapeDtypeStruct((features, width), BF16),
        scratch_shapes=[pltpu.VMEM((features, part), BF16), pltpu.SemaphoreType.DMA((part // block,))],
        input_output_aliases={1 + len(grads): 0} if started else {},
        compiler_params=kernel_params(),
        name="weight_gradient",
    )(chosen_text, *grads, *([before] if started else []))


def swap(x, axis, k):
    return lax.ppermute(x, axis, [(i, i ^ k) for i in range(lax.axis_size(axis))])


def gather_dp(x, paired):
    if not paired:
        return [lax.all_gather(x, "dp", axis=0, tiled=True)]
    near = {0: x}
    for k in range(2, lax.axis_size("dp"), 2):
        near[k] = swap(x, "dp", k)
    for k in list(near):
        near[k + 1] = swap(near[k], "dp", 1)
    return [near[k] for k in sorted(near)]


def exchange(pieces, paired):
    if paired:
        return [pieces[0]] + [swap(pieces[k], "fsdp", k) for k in range(1, len(pieces))]
    came = lax.all_to_all(jnp.stack(pieces), "fsdp", 0, 0, tiled=True)
    return [came[k] for k in range(len(pieces))]


def gather_line(first_half, second_half, both, beside):
    near_pairs = [(0, 1), (1, 0), (2, 3), (3, 2)]
    middle_pairs = [(1, 2), (2, 1)]
    outward = [(1, 0), (2, 3)]
    halves = [first_half, second_half]
    second = [swap(half, "fsdp", 2) for half in halves]
    near = lax.ppermute(both, "fsdp", near_pairs)
    second[0], beside = lax.optimization_barrier((second[0], beside))
    outer = [lax.ppermute(piece, "fsdp", outward) for piece in second]
    late, _ = lax.optimization_barrier((both, second[0]))
    inner = lax.ppermute(late, "fsdp", middle_pairs)
    parts = [[halves[i], near, second[i], inner, outer[i]] for i in range(2)]
    return parts[0], parts[1], beside


def shards(
    queries, grad_out, text_cache, w_kv, image_counts, caption_lens, caption_owner, caption_offset
):
    groups = lax.axis_size("fsdp")
    line = groups == 4
    paired = line
    dp_paired = power_of_two(lax.axis_size("dp")) and lax.axis_size("dp") <= 8
    depth = text_cache.shape[0]
    each = depth // groups
    width = queries.shape[1]

    partials = project(groups, paired, text_cache, w_kv)
    came = exchange(partials, paired)
    table = scalar_table(image_counts, caption_lens, caption_owner, caption_offset)
    rows = sum(piece.astype(F32) for piece in came).astype(BF16)
    class_rows = gather_dp(rows, dp_paired)
    outgoing = select_rows(groups, each, paired, dp_paired, table, class_rows)
    keys_values = exchange(outgoing, paired)
    probs, _, grad_values = value_grads(groups, each, paired, table, queries, grad_out, keys_values)
    grad_values, probs = lax.optimization_barrier((grad_values, probs))
    grad_query, grad_keys, grad_both = key_grads(groups, probs, queries, grad_out, grad_values, keys_values)
    grad_keys, grad_both, late_cache = lax.optimization_barrier((grad_keys, grad_both, text_cache))
    texts = [lax.all_gather(late_cache, "dp", axis=0, tiled=True)]
    chosen_text = slot_texts(groups, each, depth, paired, False, table, texts)
    if line:
        value_parts, key_parts, chosen_text = gather_line(grad_values, grad_keys, grad_both, chosen_text)
    else:
        value_parts, key_parts = [
            [lax.all_gather(half, "fsdp", axis=0, tiled=True)] for half in (grad_values, grad_keys)
        ]
    value_parts, key_parts = lax.optimization_barrier((value_parts, key_parts))
    grad_weight = weight_grad(line, chosen_text, value_parts, 2 * width, width)
    grad_weight = weight_grad(line, chosen_text, key_parts, 2 * width, 0, grad_weight)
    return grad_query, grad_weight[None]


def solution(mesh):
    in_specs = (
        P(("dp", "fsdp"), None),
        P(("dp", "fsdp"), None),
        P("dp", "fsdp"),
        P("fsdp", None),
        P(("dp", "fsdp"), None),
        P("dp", None),
        P("dp", None),
        P("dp", None),
    )
    out_specs = (P(("dp", "fsdp"), None), P("dp", "fsdp", None))
    return jax.shard_map(shards, mesh=mesh, in_specs=in_specs, out_specs=out_specs, check_vma=False)
```

```python
import functools

import jax
import jax.numpy as jnp
from jax import lax
from jax.experimental import pallas as pl
from jax.experimental.pallas import tpu as pltpu
from jax.sharding import PartitionSpec as P

HEADS = 12
HEAD = 128
LMAX = 32
SAMPLES = 2
VMEM = 48 * 1024 * 1024

F32 = jnp.float32
BF16 = jnp.bfloat16


def power_of_two(n):
    return n & (n - 1) == 0


def kernel_params(**more):
    return pltpu.CompilerParams(vmem_limit_bytes=VMEM, **more)


SMEM_SPEC = pl.BlockSpec(memory_space=pltpu.SMEM)
VMEM_SPEC = pl.BlockSpec(memory_space=pltpu.VMEM)
ANY_SPEC = pl.BlockSpec(memory_space=pl.ANY)
HBM_SPEC = pl.BlockSpec(memory_space=pltpu.HBM)


def scalar_table(image_counts, caption_lens, caption_owner, caption_offset):
    captions = caption_lens.shape[1]
    place = jnp.stack([lax.axis_index("dp"), lax.axis_index("fsdp"), image_counts[0, 0]]).astype(jnp.int32)
    place = jnp.pad(place, (0, captions - place.shape[0]))
    return jnp.concatenate([caption_lens, caption_owner, caption_offset, place[None]], axis=0)


def peer(index, k, paired):
    return index ^ k if paired else k


def first_of_class(offset, residue, groups):
    return lax.div(offset - residue + groups - 1, jnp.int32(groups))


def spread_rows(values, rows_each, shape):
    rows = lax.broadcasted_iota(jnp.int32, shape, 0)
    result = jnp.zeros(shape, jnp.int32)
    for g, value in enumerate(values):
        result = jnp.where((rows >= g * rows_each) & (rows < (g + 1) * rows_each), value + rows - g * rows_each, result)
    return result


def project_kernel(groups, paired, chunks, cache, weight, *refs):
    outs = refs[:groups]
    held_cache, held_weight, cache_sem, weight_sem = refs[groups:]
    depth = cache.shape[0]
    each = depth // groups
    rows = weight.shape[0] // chunks
    cache_copy = pltpu.make_async_copy(cache, held_cache, cache_sem)
    cache_copy.start()
    copies = [
        pltpu.make_async_copy(weight.at[pl.ds(i * rows, rows)], held_weight.at[pl.ds(i * rows, rows)], weight_sem.at[i])
        for i in range(chunks)
    ]
    for copy in copies:
        copy.start()
    member = lax.axis_index("fsdp")
    row = lax.broadcasted_iota(jnp.int32, (depth, depth), 0)
    column = lax.broadcasted_iota(jnp.int32, (depth, depth), 1)
    wanted = jnp.zeros((depth, depth), jnp.int32)
    for k in range(groups):
        wanted = jnp.where(row // each == k, groups * (row - k * each) + peer(member, k, paired), wanted)
    order = (wanted == column).astype(BF16)
    cache_copy.wait()
    sorted_rows = jnp.dot(order, held_cache[...], preferred_element_type=F32).astype(BF16)
    product = None
    for i, copy in enumerate(copies):
        copy.wait()
        at = slice(i * rows, (i + 1) * rows)
        part = jnp.dot(sorted_rows[:, at], held_weight[at], preferred_element_type=F32)
        product = part if product is None else product + part
    for k in range(groups):
        outs[k][...] = product[k * each : (k + 1) * each].astype(BF16)


def project(groups, paired, text_cache, w_kv):
    depth, features = text_cache.shape
    width = w_kv.shape[1]
    chunks = features // 128
    each = depth // groups
    return pl.pallas_call(
        functools.partial(project_kernel, groups, paired, chunks),
        in_specs=[HBM_SPEC, HBM_SPEC],
        out_specs=[VMEM_SPEC] * groups,
        out_shape=[jax.ShapeDtypeStruct((each, width), BF16)] * groups,
        scratch_shapes=[
            pltpu.VMEM((depth, features), BF16),
            pltpu.VMEM((features, width), BF16),
            pltpu.SemaphoreType.DMA,
            pltpu.SemaphoreType.DMA((chunks,)),
        ],
        compiler_params=kernel_params(),
        name="project",
    )(pltpu.with_memory_space_constraint(text_cache, pltpu.HBM), w_kv)


def select_kernel(groups, each, paired, dp_paired, n_texts, table, *refs):
    texts, pieces, outs, chip_text = refs[:n_texts], refs[n_texts : -groups - 1], refs[-groups - 1 : -1], refs[-1]
    depth = texts[0].shape[0]
    for i, text in enumerate(texts):
        chip_text[i * depth : (i + 1) * depth] = text[...]
    held = jnp.concatenate([piece[...] for piece in pieces], axis=0) if len(pieces) > 1 else pieces[0][...]
    total = held.shape[0]
    index, member = table[3, 0], table[3, 1]
    wanted_rows = groups * SAMPLES * each
    starts, firsts = [], []
    for k in range(groups):
        for s in range(SAMPLES):
            caption = peer(member, k, paired) * SAMPLES + s
            first = first_of_class(table[2, caption], member, groups)
            owner = table[1, caption]
            firsts.append(first)
            starts.append((owner ^ index if dp_paired else owner) * each + first)
    shape = (wanted_rows, total)
    target = spread_rows(starts, each, shape)
    inside = spread_rows(firsts, each, shape) < each
    chosen = ((target == lax.broadcasted_iota(jnp.int32, shape, 1)) & inside).astype(BF16)
    rows = jnp.dot(chosen, held, preferred_element_type=F32).astype(BF16)
    size = SAMPLES * each
    for k in range(groups):
        outs[k][...] = rows[k * size : (k + 1) * size]


def select_rows(groups, each, paired, dp_paired, table, texts, pieces):
    width = pieces[0].shape[1]
    depth, features = texts[0].shape
    return pl.pallas_call(
        functools.partial(select_kernel, groups, each, paired, dp_paired, len(texts)),
        in_specs=[SMEM_SPEC] + [VMEM_SPEC] * (len(texts) + len(pieces)),
        out_specs=[VMEM_SPEC] * (groups + 1),
        out_shape=[jax.ShapeDtypeStruct((SAMPLES * each, width), BF16)] * groups
        + [jax.ShapeDtypeStruct((len(texts) * depth, features), BF16)],
        compiler_params=kernel_params(),
        name="select_rows",
    )(table, *texts, *pieces)


LAST = (((1,), (1,)), ((), ()))
FIRST = (((0,), (0,)), ((), ()))


def value_grad_kernel(groups, each, paired, table, queries, cotangent, *refs):
    pieces, (probs, probs_rounded, grad_values, scores) = refs[:groups], refs[groups:]
    tokens, width = queries.shape
    slots = groups * SAMPLES * each
    heads = width // HEAD
    member = table[3, 1]
    split = table[3, 2]
    shape = (slots, tokens)
    rows = lax.broadcasted_iota(jnp.int32, shape, 0)
    position = jnp.zeros(shape, jnp.int32)
    length = jnp.zeros(shape, jnp.int32)
    sample = jnp.zeros(shape, jnp.int32)
    for c in range(groups):
        residue = peer(member, c, paired)
        for s in range(SAMPLES):
            caption = member * SAMPLES + s
            run = (c * SAMPLES + s) * each
            here = (rows >= run) & (rows < run + each)
            first = first_of_class(table[2, caption], residue, groups)
            position = jnp.where(here, groups * (first + rows - run) + residue - table[2, caption], position)
            length = jnp.where(here, table[0, caption], length)
            sample = jnp.where(here, s, sample)
    token_sample = (lax.broadcasted_iota(jnp.int32, shape, 1) >= split).astype(jnp.int32)
    allowed = (position < length) & (sample == token_sample)
    for h in range(heads):
        at = slice(h * HEAD, (h + 1) * HEAD)
        k = jnp.concatenate([piece[:, at] for piece in pieces], axis=0)
        scores[h] = lax.dot_general(k, queries[:, at], LAST, preferred_element_type=F32)
    for h in range(heads):
        masked = jnp.where(allowed, scores[h] * HEAD ** (-0.5), F32(-1e30))
        expon = jnp.exp(masked - jnp.max(masked, axis=0, keepdims=True))
        prob = expon / jnp.sum(expon, axis=0, keepdims=True)
        probs[h] = prob
        probs_rounded[h] = prob.astype(BF16)
    for h in range(heads):
        at = slice(h * HEAD, (h + 1) * HEAD)
        grad_values[:, at] = jnp.dot(probs_rounded[h], cotangent[:, at], preferred_element_type=F32).astype(BF16)


def value_grads(groups, each, paired, table, queries, grad_out, pieces):
    tokens, width = queries.shape
    slots = groups * SAMPLES * each
    heads = width // HEAD
    return pl.pallas_call(
        functools.partial(value_grad_kernel, groups, each, paired),
        in_specs=[SMEM_SPEC] + [VMEM_SPEC] * (2 + groups),
        out_specs=[VMEM_SPEC] * 3,
        out_shape=[
            jax.ShapeDtypeStruct((heads, slots, tokens), F32),
            jax.ShapeDtypeStruct((heads, slots, tokens), BF16),
            jax.ShapeDtypeStruct((slots, width), BF16),
        ],
        scratch_shapes=[pltpu.VMEM((heads, slots, tokens), F32)],
        compiler_params=kernel_params(),
        name="value_gradients",
    )(table, queries, grad_out, *pieces)


def key_grad_kernel(groups, probs, queries, cotangent, grad_values, *refs):
    pieces, (grad_query, grad_keys, grad_both, prob_grads, score_grads) = refs[:groups], refs[groups:]
    width = queries.shape[1]
    heads = width // HEAD
    scale = HEAD ** (-0.5)
    for h in range(heads):
        values_at = slice(width + h * HEAD, width + (h + 1) * HEAD)
        v = jnp.concatenate([piece[:, values_at] for piece in pieces], axis=0)
        prob_grads[h] = lax.dot_general(v, cotangent[:, h * HEAD : (h + 1) * HEAD], LAST, preferred_element_type=F32)
    for h in range(heads):
        prob, prob_grad = probs[h], prob_grads[h]
        centre = jnp.sum(prob * prob_grad, axis=0, keepdims=True)
        score_grads[h] = (prob * (prob_grad - centre)).astype(BF16)
    for h in range(heads):
        at = slice(h * HEAD, (h + 1) * HEAD)
        k = jnp.concatenate([piece[:, at] for piece in pieces], axis=0)
        score_grad = score_grads[h]
        grad_key = (jnp.dot(score_grad, queries[:, at], preferred_element_type=F32) * scale).astype(BF16)
        grad_keys[:, at] = grad_key
        grad_both[:, at] = grad_key
        grad_query[:, at] = (lax.dot_general(score_grad, k, FIRST, preferred_element_type=F32) * scale).astype(BF16)
    grad_both[:, width:] = grad_values[...]


def key_grads(groups, probs, queries, grad_out, grad_values, pieces):
    tokens, width = queries.shape
    heads, slots, _ = probs.shape
    return pl.pallas_call(
        functools.partial(key_grad_kernel, groups),
        in_specs=[VMEM_SPEC] * (4 + groups),
        out_specs=[VMEM_SPEC] * 3,
        out_shape=[
            jax.ShapeDtypeStruct((tokens, width), BF16),
            jax.ShapeDtypeStruct((slots, width), BF16),
            jax.ShapeDtypeStruct((slots, 2 * width), BF16),
        ],
        scratch_shapes=[pltpu.VMEM((heads, slots, tokens), F32), pltpu.VMEM((heads, slots, tokens), BF16)],
        compiler_params=kernel_params(),
        name="key_gradients",
    )(probs, queries, grad_out, grad_values, *pieces)


def text_kernel(groups, each, depth, paired, dp_paired, table, text, out):
    index, member = table[3, 0], table[3, 1]
    shape = (text.shape[0], out.shape[1])
    columns = lax.broadcasted_iota(jnp.int32, shape, 1)
    runs, place = columns // each, columns % each
    target = jnp.zeros(shape, jnp.int32)
    limit = jnp.zeros(shape, jnp.int32)
    run = 0
    for k in range(groups):
        device = peer(member, k, paired)
        for c in range(groups):
            residue = peer(device, c, paired)
            for s in range(SAMPLES):
                caption = device * SAMPLES + s
                offset = table[2, caption]
                owner = table[1, caption]
                if dp_paired:
                    owner = owner - (owner & 1) + ((owner ^ index) & 1)
                base = owner * depth
                here = runs == run
                target = jnp.where(here, base + groups * first_of_class(offset, residue, groups) + residue, target)
                limit = jnp.where(here, base + offset + table[0, caption], limit)
                run += 1
    target = target + groups * place
    chosen = ((target == lax.broadcasted_iota(jnp.int32, shape, 0)) & (target < limit)).astype(BF16)
    out[...] = lax.dot_general(text[...], chosen, FIRST, preferred_element_type=F32).astype(BF16)


def slot_texts(groups, each, depth, paired, dp_paired, table, text):
    features = text.shape[1]
    return pl.pallas_call(
        functools.partial(text_kernel, groups, each, depth, paired, dp_paired),
        in_specs=[SMEM_SPEC, VMEM_SPEC],
        out_specs=VMEM_SPEC,
        out_shape=jax.ShapeDtypeStruct((features, groups * groups * SAMPLES * each), BF16),
        compiler_params=kernel_params(),
        name="slot_texts",
    )(table, text)


def weight_kernel(line, blocks, *refs):
    chosen_text, *grads = refs[:-4]
    out, every, built, sems = refs[-4:]
    halves = [grads[: len(grads) // 2], grads[len(grads) // 2 :]]
    width = every.shape[1] // 2
    if line:
        member = lax.axis_index("fsdp")
        is_inner = (member == 1) | (member == 2)
        each = every.shape[0] // 4
    for i, half in enumerate(halves):
        at = slice(i * width, (i + 1) * width)
        if line:
            own, near, second, inner, outer = half
            every[0:each, at] = own[...]
            every[each : 2 * each, at] = near[:, at]
            every[2 * each : 3 * each, at] = second[...]
            every[3 * each :, at] = jnp.where(is_inner, inner[:, at], outer[...])
        else:
            every[:, at] = half[0][...]
    rows = built.shape[0] // blocks
    copies = []
    for i in range(blocks):
        at = slice(i * rows, (i + 1) * rows)
        built[at] = jnp.dot(chosen_text[at], every[...], preferred_element_type=F32).astype(BF16)
        copy = pltpu.make_async_copy(built.at[pl.ds(i * rows, rows)], out.at[pl.ds(i * rows, rows)], sems.at[i])
        copy.start()
        copies.append(copy)
    for copy in copies:
        copy.wait()


def weight_grad(line, chosen_text, first_parts, second_parts):
    features, slots = chosen_text.shape
    width = first_parts[0].shape[1] * 2
    grads = [*first_parts, *second_parts]
    blocks = 8
    return pl.pallas_call(
        functools.partial(weight_kernel, line, blocks),
        in_specs=[VMEM_SPEC] * (1 + len(grads)),
        out_specs=ANY_SPEC,
        out_shape=jax.ShapeDtypeStruct((features, width), BF16),
        scratch_shapes=[
            pltpu.VMEM((slots, width), BF16),
            pltpu.VMEM((features, width), BF16),
            pltpu.SemaphoreType.DMA((blocks,)),
        ],
        compiler_params=kernel_params(),
        name="weight_gradient",
    )(chosen_text, *grads)


def swap(x, axis, k):
    return lax.ppermute(x, axis, [(i, i ^ k) for i in range(lax.axis_size(axis))])


def gather_dp(x, paired):
    if not paired:
        return [lax.all_gather(x, "dp", axis=0, tiled=True)]
    near = {0: x}
    for k in range(2, lax.axis_size("dp"), 2):
        near[k] = swap(x, "dp", k)
    for k in list(near):
        near[k + 1] = swap(near[k], "dp", 1)
    return [near[k] for k in sorted(near)]


def gather_chips(x):
    size = lax.axis_size("dp")
    cores = [list(range(core, size, 2)) for core in range(2)]
    return lax.all_gather(x, "dp", axis=0, tiled=True, axis_index_groups=cores)


def exchange(pieces, paired):
    if paired:
        far_first = {k: swap(pieces[k], "fsdp", k) for k in (*range(2, len(pieces)), 1)}
        return [pieces[0]] + [far_first[k] for k in range(1, len(pieces))]
    came = lax.all_to_all(jnp.stack(pieces), "fsdp", 0, 0, tiled=True)
    return [came[k] for k in range(len(pieces))]


def gather_line(first_half, second_half, both, beside):
    near_pairs = [(0, 1), (1, 0), (2, 3), (3, 2)]
    middle_pairs = [(1, 2), (2, 1)]
    outward = [(1, 0), (2, 3)]
    halves = [first_half, second_half]
    second = [swap(half, "fsdp", 2) for half in halves]
    near = lax.ppermute(both, "fsdp", near_pairs)
    second[0], beside = lax.optimization_barrier((second[0], beside))
    outer = [lax.ppermute(piece, "fsdp", outward) for piece in second]
    late, _ = lax.optimization_barrier((both, second[0]))
    inner = lax.ppermute(late, "fsdp", middle_pairs)
    parts = [[halves[i], near, second[i], inner, outer[i]] for i in range(2)]
    return parts[0], parts[1], beside


def shards(
    queries, grad_out, text_cache, w_kv, image_counts, caption_lens, caption_owner, caption_offset
):
    groups = lax.axis_size("fsdp")
    line = groups == 4
    paired = line
    dp_paired = power_of_two(lax.axis_size("dp")) and lax.axis_size("dp") <= 8
    depth = text_cache.shape[0]
    each = depth // groups
    width = queries.shape[1]

    partials = project(groups, paired, text_cache, w_kv)
    partials, late_cache = lax.optimization_barrier((partials, text_cache))
    texts = [late_cache, swap(late_cache, "dp", 1)] if dp_paired else [late_cache]
    came = exchange(partials, paired)
    table = scalar_table(image_counts, caption_lens, caption_owner, caption_offset)
    rows = sum(piece.astype(F32) for piece in came).astype(BF16)
    class_rows = gather_dp(rows, dp_paired)
    *outgoing, chip_text = select_rows(groups, each, paired, dp_paired, table, texts, class_rows)
    keys_values = exchange(outgoing, paired)
    probs, _, grad_values = value_grads(groups, each, paired, table, queries, grad_out, keys_values)
    grad_values, probs = lax.optimization_barrier((grad_values, probs))
    grad_query, grad_keys, grad_both = key_grads(groups, probs, queries, grad_out, grad_values, keys_values)
    grad_keys, grad_both, chip_text = lax.optimization_barrier((grad_keys, grad_both, chip_text))
    if dp_paired:
        text = gather_chips(chip_text)
    else:
        text = lax.all_gather(chip_text, "dp", axis=0, tiled=True)
    if line:
        value_parts, key_parts, text = gather_line(grad_values, grad_keys, grad_both, text)
    else:
        value_parts, key_parts = [
            [lax.all_gather(half, "fsdp", axis=0, tiled=True)] for half in (grad_values, grad_keys)
        ]
    chosen_text = slot_texts(groups, each, depth, paired, dp_paired, table, text)
    grad_weight = weight_grad(line, chosen_text, key_parts, value_parts)
    return grad_query, grad_weight[None]


def solution(mesh):
    in_specs = (
        P(("dp", "fsdp"), None),
        P(("dp", "fsdp"), None),
        P("dp", "fsdp"),
        P("fsdp", None),
        P(("dp", "fsdp"), None),
        P("dp", None),
        P("dp", None),
        P("dp", None),
    )
    out_specs = (P(("dp", "fsdp"), None), P("dp", "fsdp", None))
    return jax.shard_map(shards, mesh=mesh, in_specs=in_specs, out_specs=out_specs, check_vma=False)
```

```python
import functools

import jax
import jax.numpy as jnp
from jax import lax
from jax.experimental import pallas as pl
from jax.experimental.pallas import tpu as pltpu
from jax.sharding import PartitionSpec as P

HEADS = 12
HEAD = 128
LMAX = 32
SAMPLES = 2
VMEM = 48 * 1024 * 1024

F32 = jnp.float32
BF16 = jnp.bfloat16


def power_of_two(n):
    return n & (n - 1) == 0


def kernel_params(**more):
    return pltpu.CompilerParams(vmem_limit_bytes=VMEM, **more)


SMEM_SPEC = pl.BlockSpec(memory_space=pltpu.SMEM)
VMEM_SPEC = pl.BlockSpec(memory_space=pltpu.VMEM)
ANY_SPEC = pl.BlockSpec(memory_space=pl.ANY)
HBM_SPEC = pl.BlockSpec(memory_space=pltpu.HBM)


def scalar_table(image_counts, caption_lens, caption_owner, caption_offset):
    captions = caption_lens.shape[1]
    place = jnp.stack([lax.axis_index("dp"), lax.axis_index("fsdp"), image_counts[0, 0]]).astype(jnp.int32)
    place = jnp.pad(place, (0, captions - place.shape[0]))
    return jnp.concatenate([caption_lens, caption_owner, caption_offset, place[None]], axis=0)


def peer(index, k, paired):
    return index ^ k if paired else k


def first_of_class(offset, residue, groups):
    return lax.div(offset - residue + groups - 1, jnp.int32(groups))


def spread_rows(values, rows_each, shape):
    rows = lax.broadcasted_iota(jnp.int32, shape, 0)
    result = jnp.zeros(shape, jnp.int32)
    for g, value in enumerate(values):
        result = jnp.where((rows >= g * rows_each) & (rows < (g + 1) * rows_each), value + rows - g * rows_each, result)
    return result


def project_kernel(groups, paired, chunks, cache, weight, *refs):
    outs = refs[:groups]
    held_cache, held_weight, cache_sem, weight_sem = refs[groups:]
    depth = cache.shape[0]
    each = depth // groups
    rows = weight.shape[0] // chunks
    cache_copy = pltpu.make_async_copy(cache, held_cache, cache_sem)
    cache_copy.start()
    copies = [
        pltpu.make_async_copy(weight.at[pl.ds(i * rows, rows)], held_weight.at[pl.ds(i * rows, rows)], weight_sem.at[i])
        for i in range(chunks)
    ]
    for copy in copies:
        copy.start()
    member = lax.axis_index("fsdp")
    row = lax.broadcasted_iota(jnp.int32, (depth, depth), 0)
    column = lax.broadcasted_iota(jnp.int32, (depth, depth), 1)
    wanted = jnp.zeros((depth, depth), jnp.int32)
    for k in range(groups):
        wanted = jnp.where(row // each == k, groups * (row - k * each) + peer(member, k, paired), wanted)
    order = (wanted == column).astype(BF16)
    cache_copy.wait()
    sorted_rows = jnp.dot(order, held_cache[...], preferred_element_type=F32).astype(BF16)
    product = None
    for i, copy in enumerate(copies):
        copy.wait()
        at = slice(i * rows, (i + 1) * rows)
        part = jnp.dot(sorted_rows[:, at], held_weight[at], preferred_element_type=F32)
        product = part if product is None else product + part
    for k in range(groups):
        outs[k][...] = product[k * each : (k + 1) * each].astype(BF16)


def project(groups, paired, text_cache, w_kv):
    depth, features = text_cache.shape
    width = w_kv.shape[1]
    chunks = features // 128
    each = depth // groups
    return pl.pallas_call(
        functools.partial(project_kernel, groups, paired, chunks),
        in_specs=[HBM_SPEC, HBM_SPEC],
        out_specs=[VMEM_SPEC] * groups,
        out_shape=[jax.ShapeDtypeStruct((each, width), BF16)] * groups,
        scratch_shapes=[
            pltpu.VMEM((depth, features), BF16),
            pltpu.VMEM((features, width), BF16),
            pltpu.SemaphoreType.DMA,
            pltpu.SemaphoreType.DMA((chunks,)),
        ],
        compiler_params=kernel_params(),
        name="project",
    )(pltpu.with_memory_space_constraint(text_cache, pltpu.HBM), w_kv)


def select_kernel(groups, each, paired, dp_paired, n_texts, table, *refs):
    texts, pieces, outs, chip_text = refs[:n_texts], refs[n_texts : -2 * groups - 1], refs[-2 * groups - 1 : -1], refs[-1]
    depth = texts[0].shape[0]
    for i, text in enumerate(texts):
        chip_text[i * depth : (i + 1) * depth] = text[...]
    held = jnp.concatenate([piece[...] for piece in pieces], axis=0) if len(pieces) > 1 else pieces[0][...]
    total = held.shape[0]
    index, member = table[3, 0], table[3, 1]
    wanted_rows = groups * SAMPLES * each
    starts, firsts = [], []
    for k in range(groups):
        for s in range(SAMPLES):
            caption = peer(member, k, paired) * SAMPLES + s
            first = first_of_class(table[2, caption], member, groups)
            owner = table[1, caption]
            firsts.append(first)
            starts.append((owner ^ index if dp_paired else owner) * each + first)
    shape = (wanted_rows, total)
    target = spread_rows(starts, each, shape)
    inside = spread_rows(firsts, each, shape) < each
    chosen = ((target == lax.broadcasted_iota(jnp.int32, shape, 1)) & inside).astype(BF16)
    rows = jnp.dot(chosen, held, preferred_element_type=F32).astype(BF16)
    size, width = SAMPLES * each, rows.shape[1] // 2
    for k in range(groups):
        outs[k][...] = rows[k * size : (k + 1) * size, :width]
        outs[groups + k][...] = rows[k * size : (k + 1) * size, width:]


def select_rows(groups, each, paired, dp_paired, table, texts, pieces):
    width = pieces[0].shape[1]
    depth, features = texts[0].shape
    return pl.pallas_call(
        functools.partial(select_kernel, groups, each, paired, dp_paired, len(texts)),
        in_specs=[SMEM_SPEC] + [VMEM_SPEC] * (len(texts) + len(pieces)),
        out_specs=[VMEM_SPEC] * (2 * groups + 1),
        out_shape=[jax.ShapeDtypeStruct((SAMPLES * each, width // 2), BF16)] * (2 * groups)
        + [jax.ShapeDtypeStruct((len(texts) * depth, features), BF16)],
        compiler_params=kernel_params(),
        name="select_rows",
    )(table, *texts, *pieces)


LAST = (((1,), (1,)), ((), ()))
FIRST = (((0,), (0,)), ((), ()))


def value_grad_kernel(groups, each, paired, table, queries, cotangent, *refs):
    pieces, (probs, grad_values, scores, probs_rounded) = refs[:groups], refs[groups:]
    tokens, width = queries.shape
    slots = groups * SAMPLES * each
    heads = width // HEAD
    member = table[3, 1]
    split = table[3, 2]
    shape = (slots, tokens)
    rows = lax.broadcasted_iota(jnp.int32, shape, 0)
    position = jnp.zeros(shape, jnp.int32)
    length = jnp.zeros(shape, jnp.int32)
    sample = jnp.zeros(shape, jnp.int32)
    for c in range(groups):
        residue = peer(member, c, paired)
        for s in range(SAMPLES):
            caption = member * SAMPLES + s
            run = (c * SAMPLES + s) * each
            here = (rows >= run) & (rows < run + each)
            first = first_of_class(table[2, caption], residue, groups)
            position = jnp.where(here, groups * (first + rows - run) + residue - table[2, caption], position)
            length = jnp.where(here, table[0, caption], length)
            sample = jnp.where(here, s, sample)
    token_sample = (lax.broadcasted_iota(jnp.int32, shape, 1) >= split).astype(jnp.int32)
    allowed = (position < length) & (sample == token_sample)
    for h in range(heads):
        at = slice(h * HEAD, (h + 1) * HEAD)
        k = jnp.concatenate([piece[:, at] for piece in pieces], axis=0)
        scores[h] = lax.dot_general(k, queries[:, at], LAST, preferred_element_type=F32)
    for h in range(heads):
        masked = jnp.where(allowed, scores[h] * HEAD ** (-0.5), F32(-1e30))
        expon = jnp.exp(masked - jnp.max(masked, axis=0, keepdims=True))
        prob = expon / jnp.sum(expon, axis=0, keepdims=True)
        probs[h] = prob
        probs_rounded[h] = prob.astype(BF16)
    for h in range(heads):
        at = slice(h * HEAD, (h + 1) * HEAD)
        grad_values[:, at] = jnp.dot(probs_rounded[h], cotangent[:, at], preferred_element_type=F32).astype(BF16)


def value_grads(groups, each, paired, table, queries, grad_out, pieces):
    tokens, width = queries.shape
    slots = groups * SAMPLES * each
    heads = width // HEAD
    return pl.pallas_call(
        functools.partial(value_grad_kernel, groups, each, paired),
        in_specs=[SMEM_SPEC] + [VMEM_SPEC] * (2 + groups),
        out_specs=[VMEM_SPEC] * 2,
        out_shape=[
            jax.ShapeDtypeStruct((heads, slots, tokens), F32),
            jax.ShapeDtypeStruct((slots, width), BF16),
        ],
        scratch_shapes=[pltpu.VMEM((heads, slots, tokens), F32), pltpu.VMEM((heads, slots, tokens), BF16)],
        compiler_params=kernel_params(),
        name="value_gradients",
    )(table, queries, grad_out, *pieces)


def key_grad_kernel(groups, probs, queries, cotangent, grad_values, *refs):
    values, (score_grads, grad_keys, grad_both, prob_grads) = refs[:groups], refs[groups:]
    width = queries.shape[1]
    heads = width // HEAD
    scale = HEAD ** (-0.5)
    for h in range(heads):
        at = slice(h * HEAD, (h + 1) * HEAD)
        v = jnp.concatenate([piece[:, at] for piece in values], axis=0)
        prob_grads[h] = lax.dot_general(v, cotangent[:, at], LAST, preferred_element_type=F32)
    for h in range(heads):
        prob, prob_grad = probs[h], prob_grads[h]
        centre = jnp.sum(prob * prob_grad, axis=0, keepdims=True)
        score_grads[h] = (prob * (prob_grad - centre)).astype(BF16)
    for h in range(heads):
        at = slice(h * HEAD, (h + 1) * HEAD)
        grad_key = (jnp.dot(score_grads[h], queries[:, at], preferred_element_type=F32) * scale).astype(BF16)
        grad_keys[:, at] = grad_key
        grad_both[:, at] = grad_key
    grad_both[:, width:] = grad_values[...]


def key_grads(groups, probs, queries, grad_out, grad_values, values):
    tokens, width = queries.shape
    heads, slots, _ = probs.shape
    return pl.pallas_call(
        functools.partial(key_grad_kernel, groups),
        in_specs=[VMEM_SPEC] * (4 + groups),
        out_specs=[VMEM_SPEC] * 3,
        out_shape=[
            jax.ShapeDtypeStruct((heads, slots, tokens), BF16),
            jax.ShapeDtypeStruct((slots, width), BF16),
            jax.ShapeDtypeStruct((slots, 2 * width), BF16),
        ],
        scratch_shapes=[pltpu.VMEM((heads, slots, tokens), F32)],
        compiler_params=kernel_params(),
        name="key_gradients",
    )(probs, queries, grad_out, grad_values, *values)


def text_kernel(groups, each, depth, paired, dp_paired, table, text, score_grads, *refs):
    keys, (out, grad_query) = refs[:groups], refs[groups:]
    for h in range(score_grads.shape[0]):
        at = slice(h * HEAD, (h + 1) * HEAD)
        k = jnp.concatenate([piece[:, at] for piece in keys], axis=0)
        product = lax.dot_general(score_grads[h], k, FIRST, preferred_element_type=F32)
        grad_query[:, at] = (product * HEAD ** (-0.5)).astype(BF16)
    index, member = table[3, 0], table[3, 1]
    shape = (text.shape[0], out.shape[1])
    columns = lax.broadcasted_iota(jnp.int32, shape, 1)
    runs, place = columns // each, columns % each
    target = jnp.zeros(shape, jnp.int32)
    limit = jnp.zeros(shape, jnp.int32)
    run = 0
    for k in range(groups):
        device = peer(member, k, paired)
        for c in range(groups):
            residue = peer(device, c, paired)
            for s in range(SAMPLES):
                caption = device * SAMPLES + s
                offset = table[2, caption]
                owner = table[1, caption]
                if dp_paired:
                    owner = owner - (owner & 1) + ((owner ^ index) & 1)
                base = owner * depth
                here = runs == run
                target = jnp.where(here, base + groups * first_of_class(offset, residue, groups) + residue, target)
                limit = jnp.where(here, base + offset + table[0, caption], limit)
                run += 1
    target = target + groups * place
    chosen = ((target == lax.broadcasted_iota(jnp.int32, shape, 0)) & (target < limit)).astype(BF16)
    out[...] = lax.dot_general(text[...], chosen, FIRST, preferred_element_type=F32).astype(BF16)


def slot_texts(groups, each, depth, paired, dp_paired, table, text, score_grads, keys):
    features = text.shape[1]
    return pl.pallas_call(
        functools.partial(text_kernel, groups, each, depth, paired, dp_paired),
        in_specs=[SMEM_SPEC] + [VMEM_SPEC] * (2 + groups),
        out_specs=[VMEM_SPEC] * 2,
        out_shape=[
            jax.ShapeDtypeStruct((features, groups * groups * SAMPLES * each), BF16),
            jax.ShapeDtypeStruct((score_grads.shape[2], keys[0].shape[1]), BF16),
        ],
        compiler_params=kernel_params(),
        name="slot_texts",
    )(table, text, score_grads, *keys)


def weight_kernel(line, blocks, *refs):
    chosen_text, *grads = refs[:-4]
    out, every, built, sems = refs[-4:]
    halves = [grads[: len(grads) // 2], grads[len(grads) // 2 :]]
    width = every.shape[1] // 2
    if line:
        member = lax.axis_index("fsdp")
        is_inner = (member == 1) | (member == 2)
        each = every.shape[0] // 4
    for i, half in enumerate(halves):
        at = slice(i * width, (i + 1) * width)
        if line:
            own, near, second, inner, outer = half
            every[0:each, at] = own[...]
            every[each : 2 * each, at] = near[:, at]
            every[2 * each : 3 * each, at] = second[...]
            every[3 * each :, at] = jnp.where(is_inner, inner[:, at], outer[...])
        else:
            every[:, at] = half[0][...]
    rows = built.shape[0] // blocks
    copies = []
    for i in range(blocks):
        at = slice(i * rows, (i + 1) * rows)
        built[at] = jnp.dot(chosen_text[at], every[...], preferred_element_type=F32).astype(BF16)
        copy = pltpu.make_async_copy(built.at[pl.ds(i * rows, rows)], out.at[pl.ds(i * rows, rows)], sems.at[i])
        copy.start()
        copies.append(copy)
    for copy in copies:
        copy.wait()


def weight_grad(line, chosen_text, first_parts, second_parts):
    features, slots = chosen_text.shape
    width = first_parts[0].shape[1] * 2
    grads = [*first_parts, *second_parts]
    blocks = 8
    return pl.pallas_call(
        functools.partial(weight_kernel, line, blocks),
        in_specs=[VMEM_SPEC] * (1 + len(grads)),
        out_specs=ANY_SPEC,
        out_shape=jax.ShapeDtypeStruct((features, width), BF16),
        scratch_shapes=[
            pltpu.VMEM((slots, width), BF16),
            pltpu.VMEM((features, width), BF16),
            pltpu.SemaphoreType.DMA((blocks,)),
        ],
        compiler_params=kernel_params(),
        name="weight_gradient",
    )(chosen_text, *grads)


def swap(x, axis, k):
    return lax.ppermute(x, axis, [(i, i ^ k) for i in range(lax.axis_size(axis))])


def gather_dp(x, paired):
    if not paired:
        return [lax.all_gather(x, "dp", axis=0, tiled=True)]
    near = {0: x}
    for k in range(2, lax.axis_size("dp"), 2):
        near[k] = swap(x, "dp", k)
    for k in list(near):
        near[k + 1] = swap(near[k], "dp", 1)
    return [near[k] for k in sorted(near)]


def gather_chips(x):
    size = lax.axis_size("dp")
    cores = [list(range(core, size, 2)) for core in range(2)]
    return lax.all_gather(x, "dp", axis=0, tiled=True, axis_index_groups=cores)


def exchange(pieces, paired):
    if paired:
        far_first = {k: swap(pieces[k], "fsdp", k) for k in (*range(2, len(pieces)), 1)}
        return [pieces[0]] + [far_first[k] for k in range(1, len(pieces))]
    came = lax.all_to_all(jnp.stack(pieces), "fsdp", 0, 0, tiled=True)
    return [came[k] for k in range(len(pieces))]


def gather_line(first_half, second_half, both, beside):
    near_pairs = [(0, 1), (1, 0), (2, 3), (3, 2)]
    middle_pairs = [(1, 2), (2, 1)]
    outward = [(1, 0), (2, 3)]
    halves = [first_half, second_half]
    second = [swap(half, "fsdp", 2) for half in halves]
    near = lax.ppermute(both, "fsdp", near_pairs)
    second[0], beside = lax.optimization_barrier((second[0], beside))
    outer = [lax.ppermute(piece, "fsdp", outward) for piece in second]
    late, _ = lax.optimization_barrier((both, second[0]))
    inner = lax.ppermute(late, "fsdp", middle_pairs)
    parts = [[halves[i], near, second[i], inner, outer[i]] for i in range(2)]
    return parts[0], parts[1], beside


def shards(
    queries, grad_out, text_cache, w_kv, image_counts, caption_lens, caption_owner, caption_offset
):
    groups = lax.axis_size("fsdp")
    line = groups == 4
    paired = line
    dp_paired = power_of_two(lax.axis_size("dp")) and lax.axis_size("dp") <= 8
    depth = text_cache.shape[0]
    each = depth // groups
    width = queries.shape[1]

    partials = project(groups, paired, text_cache, w_kv)
    partials, late_cache = lax.optimization_barrier((partials, text_cache))
    texts = [late_cache, swap(late_cache, "dp", 1)] if dp_paired else [late_cache]
    came = exchange(partials, paired)
    table = scalar_table(image_counts, caption_lens, caption_owner, caption_offset)
    rows = sum(piece.astype(F32) for piece in came).astype(BF16)
    class_rows = gather_dp(rows, dp_paired)
    *outgoing, chip_text = select_rows(groups, each, paired, dp_paired, table, texts, class_rows)
    keys = exchange(outgoing[:groups], paired)
    values = exchange(outgoing[groups:], paired)
    probs, grad_values = value_grads(groups, each, paired, table, queries, grad_out, keys)
    grad_values, probs = lax.optimization_barrier((grad_values, probs))
    score_grads, grad_keys, grad_both = key_grads(groups, probs, queries, grad_out, grad_values, values)
    grad_values, grad_keys, grad_both, chip_text = lax.optimization_barrier(
        (grad_values, grad_keys, grad_both, chip_text)
    )
    if dp_paired:
        text = gather_chips(chip_text)
    else:
        text = lax.all_gather(chip_text, "dp", axis=0, tiled=True)
    if line:
        value_parts, key_parts, text = gather_line(grad_values, grad_keys, grad_both, text)
    else:
        value_parts, key_parts = [
            [lax.all_gather(half, "fsdp", axis=0, tiled=True)] for half in (grad_values, grad_keys)
        ]
    chosen_text, grad_query = slot_texts(groups, each, depth, paired, dp_paired, table, text, score_grads, keys)
    grad_weight = weight_grad(line, chosen_text, key_parts, value_parts)
    return grad_query, grad_weight[None]


def solution(mesh):
    in_specs = (
        P(("dp", "fsdp"), None),
        P(("dp", "fsdp"), None),
        P("dp", "fsdp"),
        P("fsdp", None),
        P(("dp", "fsdp"), None),
        P("dp", None),
        P("dp", None),
        P("dp", None),
    )
    out_specs = (P(("dp", "fsdp"), None), P("dp", "fsdp", None))
    return jax.shard_map(shards, mesh=mesh, in_specs=in_specs, out_specs=out_specs, check_vma=False)
```

```python
import functools

import jax
import jax.numpy as jnp
from jax import lax
from jax.experimental import pallas as pl
from jax.experimental.pallas import tpu as pltpu
from jax.sharding import PartitionSpec as P

HEADS = 12
HEAD = 128
LMAX = 32
SAMPLES = 2
VMEM = 48 * 1024 * 1024

F32 = jnp.float32
BF16 = jnp.bfloat16


def power_of_two(n):
    return n & (n - 1) == 0


def kernel_params(**more):
    return pltpu.CompilerParams(vmem_limit_bytes=VMEM, **more)


SMEM_SPEC = pl.BlockSpec(memory_space=pltpu.SMEM)
VMEM_SPEC = pl.BlockSpec(memory_space=pltpu.VMEM)
ANY_SPEC = pl.BlockSpec(memory_space=pl.ANY)
HBM_SPEC = pl.BlockSpec(memory_space=pltpu.HBM)


def scalar_table(image_counts, caption_lens, caption_owner, caption_offset):
    captions = caption_lens.shape[1]
    place = jnp.stack([lax.axis_index("dp"), lax.axis_index("fsdp"), image_counts[0, 0]]).astype(jnp.int32)
    place = jnp.pad(place, (0, captions - place.shape[0]))
    return jnp.concatenate([caption_lens, caption_owner, caption_offset, place[None]], axis=0)


def peer(index, k, paired):
    return index ^ k if paired else k


def first_of_class(offset, residue, groups):
    return lax.div(offset - residue + groups - 1, jnp.int32(groups))


def spread_rows(values, rows_each, shape):
    rows = lax.broadcasted_iota(jnp.int32, shape, 0)
    result = jnp.zeros(shape, jnp.int32)
    for g, value in enumerate(values):
        result = jnp.where((rows >= g * rows_each) & (rows < (g + 1) * rows_each), value + rows - g * rows_each, result)
    return result


def project_kernel(groups, paired, chunks, cache, weight, *refs):
    outs = refs[:groups]
    held_cache, held_weight, cache_sem, weight_sem = refs[groups:]
    depth = cache.shape[0]
    each = depth // groups
    rows = weight.shape[0] // chunks
    cache_copy = pltpu.make_async_copy(cache, held_cache, cache_sem)
    cache_copy.start()
    copies = [
        pltpu.make_async_copy(weight.at[pl.ds(i * rows, rows)], held_weight.at[pl.ds(i * rows, rows)], weight_sem.at[i])
        for i in range(chunks)
    ]
    for copy in copies:
        copy.start(priority=1)
    member = lax.axis_index("fsdp")
    row = lax.broadcasted_iota(jnp.int32, (depth, depth), 0)
    column = lax.broadcasted_iota(jnp.int32, (depth, depth), 1)
    wanted = jnp.zeros((depth, depth), jnp.int32)
    for k in range(groups):
        wanted = jnp.where(row // each == k, groups * (row - k * each) + peer(member, k, paired), wanted)
    order = (wanted == column).astype(BF16)
    cache_copy.wait()
    sorted_rows = jnp.dot(order, held_cache[...], preferred_element_type=F32).astype(BF16)
    product = None
    for i, copy in enumerate(copies):
        copy.wait()
        at = slice(i * rows, (i + 1) * rows)
        part = jnp.dot(sorted_rows[:, at], held_weight[at], preferred_element_type=F32)
        product = part if product is None else product + part
    for k in range(groups):
        outs[k][...] = product[k * each : (k + 1) * each].astype(BF16)


def project(groups, paired, text_cache, w_kv):
    depth, features = text_cache.shape
    width = w_kv.shape[1]
    chunks = features // 128
    each = depth // groups
    return pl.pallas_call(
        functools.partial(project_kernel, groups, paired, chunks),
        in_specs=[HBM_SPEC, HBM_SPEC],
        out_specs=[VMEM_SPEC] * groups,
        out_shape=[jax.ShapeDtypeStruct((each, width), BF16)] * groups,
        scratch_shapes=[
            pltpu.VMEM((depth, features), BF16),
            pltpu.VMEM((features, width), BF16),
            pltpu.SemaphoreType.DMA,
            pltpu.SemaphoreType.DMA((chunks,)),
        ],
        compiler_params=kernel_params(),
        name="project",
    )(pltpu.with_memory_space_constraint(text_cache, pltpu.HBM), w_kv)


def select_kernel(groups, each, paired, dp_paired, n_texts, table, *refs):
    texts, pieces, outs, chip_text = refs[:n_texts], refs[n_texts : -2 * groups - 1], refs[-2 * groups - 1 : -1], refs[-1]
    depth = texts[0].shape[0]
    for i, text in enumerate(texts):
        chip_text[i * depth : (i + 1) * depth] = text[...]
    held = jnp.concatenate([piece[...] for piece in pieces], axis=0) if len(pieces) > 1 else pieces[0][...]
    total = held.shape[0]
    index, member = table[3, 0], table[3, 1]
    wanted_rows = groups * SAMPLES * each
    starts, firsts = [], []
    for k in range(groups):
        for s in range(SAMPLES):
            caption = peer(member, k, paired) * SAMPLES + s
            first = first_of_class(table[2, caption], member, groups)
            owner = table[1, caption]
            firsts.append(first)
            starts.append((owner ^ index if dp_paired else owner) * each + first)
    shape = (wanted_rows, total)
    target = spread_rows(starts, each, shape)
    inside = spread_rows(firsts, each, shape) < each
    chosen = ((target == lax.broadcasted_iota(jnp.int32, shape, 1)) & inside).astype(BF16)
    rows = jnp.dot(chosen, held, preferred_element_type=F32).astype(BF16)
    size, width = SAMPLES * each, rows.shape[1] // 2
    for k in range(groups):
        outs[k][...] = rows[k * size : (k + 1) * size, :width]
        outs[groups + k][...] = rows[k * size : (k + 1) * size, width:]


def select_rows(groups, each, paired, dp_paired, table, texts, pieces):
    width = pieces[0].shape[1]
    depth, features = texts[0].shape
    return pl.pallas_call(
        functools.partial(select_kernel, groups, each, paired, dp_paired, len(texts)),
        in_specs=[SMEM_SPEC] + [VMEM_SPEC] * (len(texts) + len(pieces)),
        out_specs=[VMEM_SPEC] * (2 * groups + 1),
        out_shape=[jax.ShapeDtypeStruct((SAMPLES * each, width // 2), BF16)] * (2 * groups)
        + [jax.ShapeDtypeStruct((len(texts) * depth, features), BF16)],
        compiler_params=kernel_params(),
        name="select_rows",
    )(table, *texts, *pieces)


LAST = (((1,), (1,)), ((), ()))
FIRST = (((0,), (0,)), ((), ()))


def value_grad_kernel(groups, each, paired, table, queries, cotangent, *refs):
    pieces, (probs, grad_values, scores, probs_rounded) = refs[:groups], refs[groups:]
    tokens, width = queries.shape
    slots = groups * SAMPLES * each
    heads = width // HEAD
    member = table[3, 1]
    split = table[3, 2]
    shape = (slots, tokens)
    rows = lax.broadcasted_iota(jnp.int32, shape, 0)
    position = jnp.zeros(shape, jnp.int32)
    length = jnp.zeros(shape, jnp.int32)
    sample = jnp.zeros(shape, jnp.int32)
    for c in range(groups):
        residue = peer(member, c, paired)
        for s in range(SAMPLES):
            caption = member * SAMPLES + s
            run = (c * SAMPLES + s) * each
            here = (rows >= run) & (rows < run + each)
            first = first_of_class(table[2, caption], residue, groups)
            position = jnp.where(here, groups * (first + rows - run) + residue - table[2, caption], position)
            length = jnp.where(here, table[0, caption], length)
            sample = jnp.where(here, s, sample)
    token_sample = (lax.broadcasted_iota(jnp.int32, shape, 1) >= split).astype(jnp.int32)
    allowed = (position < length) & (sample == token_sample)
    for h in range(heads):
        at = slice(h * HEAD, (h + 1) * HEAD)
        k = jnp.concatenate([piece[:, at] for piece in pieces], axis=0)
        scores[h] = lax.dot_general(k, queries[:, at], LAST, preferred_element_type=F32)
    for h in range(heads):
        masked = jnp.where(allowed, scores[h] * HEAD ** (-0.5), F32(-1e30))
        expon = jnp.exp(masked - jnp.max(masked, axis=0, keepdims=True))
        prob = expon / jnp.sum(expon, axis=0, keepdims=True)
        probs[h] = prob
        probs_rounded[h] = prob.astype(BF16)
    for h in range(heads):
        at = slice(h * HEAD, (h + 1) * HEAD)
        grad_values[:, at] = jnp.dot(probs_rounded[h], cotangent[:, at], preferred_element_type=F32).astype(BF16)


def value_grads(groups, each, paired, table, queries, grad_out, pieces):
    tokens, width = queries.shape
    slots = groups * SAMPLES * each
    heads = width // HEAD
    return pl.pallas_call(
        functools.partial(value_grad_kernel, groups, each, paired),
        in_specs=[SMEM_SPEC] + [VMEM_SPEC] * (2 + groups),
        out_specs=[VMEM_SPEC] * 2,
        out_shape=[
            jax.ShapeDtypeStruct((heads, slots, tokens), F32),
            jax.ShapeDtypeStruct((slots, width), BF16),
        ],
        scratch_shapes=[pltpu.VMEM((heads, slots, tokens), F32), pltpu.VMEM((heads, slots, tokens), BF16)],
        compiler_params=kernel_params(),
        name="value_gradients",
    )(table, queries, grad_out, *pieces)


def key_grad_kernel(groups, probs, queries, cotangent, grad_values, *refs):
    values, (score_grads, grad_keys, grad_both, prob_grads) = refs[:groups], refs[groups:]
    width = queries.shape[1]
    heads = width // HEAD
    scale = HEAD ** (-0.5)
    for h in range(heads):
        at = slice(h * HEAD, (h + 1) * HEAD)
        v = jnp.concatenate([piece[:, at] for piece in values], axis=0)
        prob_grads[h] = lax.dot_general(v, cotangent[:, at], LAST, preferred_element_type=F32)
    for h in range(heads):
        prob, prob_grad = probs[h], prob_grads[h]
        centre = jnp.sum(prob * prob_grad, axis=0, keepdims=True)
        score_grads[h] = (prob * (prob_grad - centre)).astype(BF16)
    for h in range(heads):
        at = slice(h * HEAD, (h + 1) * HEAD)
        grad_key = (jnp.dot(score_grads[h], queries[:, at], preferred_element_type=F32) * scale).astype(BF16)
        grad_keys[:, at] = grad_key
        grad_both[:, at] = grad_key
    grad_both[:, width:] = grad_values[...]


def key_grads(groups, probs, queries, grad_out, grad_values, values):
    tokens, width = queries.shape
    heads, slots, _ = probs.shape
    return pl.pallas_call(
        functools.partial(key_grad_kernel, groups),
        in_specs=[VMEM_SPEC] * (4 + groups),
        out_specs=[VMEM_SPEC] * 3,
        out_shape=[
            jax.ShapeDtypeStruct((heads, slots, tokens), BF16),
            jax.ShapeDtypeStruct((slots, width), BF16),
            jax.ShapeDtypeStruct((slots, 2 * width), BF16),
        ],
        scratch_shapes=[pltpu.VMEM((heads, slots, tokens), F32)],
        compiler_params=kernel_params(),
        name="key_gradients",
    )(probs, queries, grad_out, grad_values, *values)


def text_kernel(groups, each, depth, paired, dp_paired, table, text, score_grads, *refs):
    keys, (out, grad_query) = refs[:groups], refs[groups:]
    for h in range(score_grads.shape[0]):
        at = slice(h * HEAD, (h + 1) * HEAD)
        k = jnp.concatenate([piece[:, at] for piece in keys], axis=0)
        product = lax.dot_general(score_grads[h], k, FIRST, preferred_element_type=F32)
        grad_query[:, at] = (product * HEAD ** (-0.5)).astype(BF16)
    index, member = table[3, 0], table[3, 1]
    shape = (text.shape[0], out.shape[1])
    columns = lax.broadcasted_iota(jnp.int32, shape, 1)
    runs, place = columns // each, columns % each
    target = jnp.zeros(shape, jnp.int32)
    limit = jnp.zeros(shape, jnp.int32)
    run = 0
    for k in range(groups):
        device = peer(member, k, paired)
        for c in range(groups):
            residue = peer(device, c, paired)
            for s in range(SAMPLES):
                caption = device * SAMPLES + s
                offset = table[2, caption]
                owner = table[1, caption]
                if dp_paired:
                    owner = owner - (owner & 1) + ((owner ^ index) & 1)
                base = owner * depth
                here = runs == run
                target = jnp.where(here, base + groups * first_of_class(offset, residue, groups) + residue, target)
                limit = jnp.where(here, base + offset + table[0, caption], limit)
                run += 1
    target = target + groups * place
    chosen = ((target == lax.broadcasted_iota(jnp.int32, shape, 0)) & (target < limit)).astype(BF16)
    out[...] = lax.dot_general(text[...], chosen, FIRST, preferred_element_type=F32).astype(BF16)


def slot_texts(groups, each, depth, paired, dp_paired, table, text, score_grads, keys):
    features = text.shape[1]
    return pl.pallas_call(
        functools.partial(text_kernel, groups, each, depth, paired, dp_paired),
        in_specs=[SMEM_SPEC] + [VMEM_SPEC] * (2 + groups),
        out_specs=[VMEM_SPEC] * 2,
        out_shape=[
            jax.ShapeDtypeStruct((features, groups * groups * SAMPLES * each), BF16),
            jax.ShapeDtypeStruct((score_grads.shape[2], keys[0].shape[1]), BF16),
        ],
        compiler_params=kernel_params(),
        name="slot_texts",
    )(table, text, score_grads, *keys)


def weight_kernel(line, blocks, *refs):
    chosen_text, *grads = refs[:-4]
    out, every, built, sems = refs[-4:]
    halves = [grads[: len(grads) // 2], grads[len(grads) // 2 :]]
    width = every.shape[1] // 2
    if line:
        member = lax.axis_index("fsdp")
        is_inner = (member == 1) | (member == 2)
        each = every.shape[0] // 4
    for i, half in enumerate(halves):
        at = slice(i * width, (i + 1) * width)
        if line:
            own, near, second, inner, outer = half
            every[0:each, at] = own[...]
            every[each : 2 * each, at] = near[:, at]
            every[2 * each : 3 * each, at] = second[...]
            every[3 * each :, at] = jnp.where(is_inner, inner[:, at], outer[...])
        else:
            every[:, at] = half[0][...]
    rows = built.shape[0] // blocks
    copies = []
    for i in range(blocks):
        at = slice(i * rows, (i + 1) * rows)
        built[at] = jnp.dot(chosen_text[at], every[...], preferred_element_type=F32).astype(BF16)
        copy = pltpu.make_async_copy(built.at[pl.ds(i * rows, rows)], out.at[pl.ds(i * rows, rows)], sems.at[i])
        copy.start()
        copies.append(copy)
    for copy in copies:
        copy.wait()


def weight_grad(line, chosen_text, first_parts, second_parts):
    features, slots = chosen_text.shape
    width = first_parts[0].shape[1] * 2
    grads = [*first_parts, *second_parts]
    blocks = 8
    return pl.pallas_call(
        functools.partial(weight_kernel, line, blocks),
        in_specs=[VMEM_SPEC] * (1 + len(grads)),
        out_specs=ANY_SPEC,
        out_shape=jax.ShapeDtypeStruct((features, width), BF16),
        scratch_shapes=[
            pltpu.VMEM((slots, width), BF16),
            pltpu.VMEM((features, width), BF16),
            pltpu.SemaphoreType.DMA((blocks,)),
        ],
        compiler_params=kernel_params(),
        name="weight_gradient",
    )(chosen_text, *grads)


def swap(x, axis, k):
    return lax.ppermute(x, axis, [(i, i ^ k) for i in range(lax.axis_size(axis))])


def gather_dp(x, paired):
    if not paired:
        return [lax.all_gather(x, "dp", axis=0, tiled=True)]
    near = {0: x}
    for k in range(2, lax.axis_size("dp"), 2):
        near[k] = swap(x, "dp", k)
    for k in list(near):
        near[k + 1] = swap(near[k], "dp", 1)
    return [near[k] for k in sorted(near)]


def gather_chips(x):
    size = lax.axis_size("dp")
    cores = [list(range(core, size, 2)) for core in range(2)]
    return lax.all_gather(x, "dp", axis=0, tiled=True, axis_index_groups=cores)


def exchange(pieces, paired):
    if paired:
        far_first = {k: swap(pieces[k], "fsdp", k) for k in (*range(2, len(pieces)), 1)}
        return [pieces[0]] + [far_first[k] for k in range(1, len(pieces))]
    came = lax.all_to_all(jnp.stack(pieces), "fsdp", 0, 0, tiled=True)
    return [came[k] for k in range(len(pieces))]


def gather_line(first_half, second_half, both, beside):
    near_pairs = [(0, 1), (1, 0), (2, 3), (3, 2)]
    middle_pairs = [(1, 2), (2, 1)]
    outward = [(1, 0), (2, 3)]
    halves = [first_half, second_half]
    second = [swap(half, "fsdp", 2) for half in halves]
    near = lax.ppermute(both, "fsdp", near_pairs)
    second[0], beside = lax.optimization_barrier((second[0], beside))
    outer = [lax.ppermute(piece, "fsdp", outward) for piece in second]
    late, _ = lax.optimization_barrier((both, second[0]))
    inner = lax.ppermute(late, "fsdp", middle_pairs)
    parts = [[halves[i], near, second[i], inner, outer[i]] for i in range(2)]
    return parts[0], parts[1], beside


def shards(
    queries, grad_out, text_cache, w_kv, image_counts, caption_lens, caption_owner, caption_offset
):
    groups = lax.axis_size("fsdp")
    line = groups == 4
    paired = line
    dp_paired = power_of_two(lax.axis_size("dp")) and lax.axis_size("dp") <= 8
    depth = text_cache.shape[0]
    each = depth // groups
    width = queries.shape[1]

    partials = project(groups, paired, text_cache, w_kv)
    partials, late_cache = lax.optimization_barrier((partials, text_cache))
    texts = [late_cache, swap(late_cache, "dp", 1)] if dp_paired else [late_cache]
    came = exchange(partials, paired)
    table = scalar_table(image_counts, caption_lens, caption_owner, caption_offset)
    rows = sum(piece.astype(F32) for piece in came).astype(BF16)
    class_rows = gather_dp(rows, dp_paired)
    *outgoing, chip_text = select_rows(groups, each, paired, dp_paired, table, texts, class_rows)
    keys = exchange(outgoing[:groups], paired)
    values = exchange(outgoing[groups:], paired)
    probs, grad_values = value_grads(groups, each, paired, table, queries, grad_out, keys)
    grad_values, probs = lax.optimization_barrier((grad_values, probs))
    score_grads, grad_keys, grad_both = key_grads(groups, probs, queries, grad_out, grad_values, values)
    grad_values, grad_keys, grad_both, chip_text = lax.optimization_barrier(
        (grad_values, grad_keys, grad_both, chip_text)
    )
    if dp_paired:
        text = gather_chips(chip_text)
    else:
        text = lax.all_gather(chip_text, "dp", axis=0, tiled=True)
    if line:
        value_parts, key_parts, text = gather_line(grad_values, grad_keys, grad_both, text)
    else:
        value_parts, key_parts = [
            [lax.all_gather(half, "fsdp", axis=0, tiled=True)] for half in (grad_values, grad_keys)
        ]
    chosen_text, grad_query = slot_texts(groups, each, depth, paired, dp_paired, table, text, score_grads, keys)
    grad_weight = weight_grad(line, chosen_text, key_parts, value_parts)
    return grad_query, grad_weight[None]


def solution(mesh):
    in_specs = (
        P(("dp", "fsdp"), None),
        P(("dp", "fsdp"), None),
        P("dp", "fsdp"),
        P("fsdp", None),
        P(("dp", "fsdp"), None),
        P("dp", None),
        P("dp", None),
        P("dp", None),
    )
    out_specs = (P(("dp", "fsdp"), None), P("dp", "fsdp", None))
    return jax.shard_map(shards, mesh=mesh, in_specs=in_specs, out_specs=out_specs, check_vma=False)
```

```python
import functools

import jax
import jax.numpy as jnp
from jax import lax
from jax.experimental import pallas as pl
from jax.experimental.pallas import tpu as pltpu
from jax.sharding import PartitionSpec as P

HEADS = 12
HEAD = 128
LMAX = 32
SAMPLES = 2
FIRST_HEADS = 12
CLASSES = 4
VMEM = 48 * 1024 * 1024

F32 = jnp.float32
BF16 = jnp.bfloat16


def power_of_two(n):
    return n & (n - 1) == 0


def kernel_params(**more):
    return pltpu.CompilerParams(vmem_limit_bytes=VMEM, **more)


SMEM_SPEC = pl.BlockSpec(memory_space=pltpu.SMEM)
VMEM_SPEC = pl.BlockSpec(memory_space=pltpu.VMEM)
ANY_SPEC = pl.BlockSpec(memory_space=pl.ANY)
HBM_SPEC = pl.BlockSpec(memory_space=pltpu.HBM)


def scalar_table(image_counts, caption_lens, caption_owner, caption_offset):
    captions = caption_lens.shape[1]
    place = jnp.stack([lax.axis_index("dp"), lax.axis_index("fsdp"), image_counts[0, 0]]).astype(jnp.int32)
    place = jnp.pad(place, (0, captions - place.shape[0]))
    return jnp.concatenate([caption_lens, caption_owner, caption_offset, place[None]], axis=0)


def peer(index, k, paired):
    return index ^ k if paired else k


def residue_of(member, k, classes, paired):
    return (member ^ k) & (classes - 1) if paired else k


def own_residue(member, classes, paired):
    return member & (classes - 1) if paired else member


def first_of_class(offset, residue, groups):
    return lax.div(offset - residue + groups - 1, jnp.int32(groups))


def spread_rows(values, rows_each, shape):
    rows = lax.broadcasted_iota(jnp.int32, shape, 0)
    result = jnp.zeros(shape, jnp.int32)
    for g, value in enumerate(values):
        result = jnp.where((rows >= g * rows_each) & (rows < (g + 1) * rows_each), value + rows - g * rows_each, result)
    return result


def project_kernel(groups, paired, chunks, cache, weight, *refs):
    outs = refs[:groups]
    held_cache, held_weight, cache_sem, weight_sem = refs[groups:]
    depth = cache.shape[0]
    each = depth // groups
    rows = weight.shape[0] // chunks
    cache_copy = pltpu.make_async_copy(cache, held_cache, cache_sem)
    cache_copy.start()
    copies = [
        pltpu.make_async_copy(weight.at[pl.ds(i * rows, rows)], held_weight.at[pl.ds(i * rows, rows)], weight_sem.at[i])
        for i in range(chunks)
    ]
    for copy in copies:
        copy.start(priority=1)
    member = lax.axis_index("fsdp")
    row = lax.broadcasted_iota(jnp.int32, (depth, depth), 0)
    column = lax.broadcasted_iota(jnp.int32, (depth, depth), 1)
    wanted = jnp.zeros((depth, depth), jnp.int32)
    for k in range(groups):
        residue = residue_of(member, k, groups, paired)
        wanted = jnp.where(row // each == k, groups * (row - k * each) + residue, wanted)
    order = (wanted == column).astype(BF16)
    cache_copy.wait()
    sorted_rows = jnp.dot(order, held_cache[...], preferred_element_type=F32).astype(BF16)
    product = None
    for i, copy in enumerate(copies):
        copy.wait()
        at = slice(i * rows, (i + 1) * rows)
        part = jnp.dot(sorted_rows[:, at], held_weight[at], preferred_element_type=F32)
        product = part if product is None else product + part
    for k in range(groups):
        outs[k][...] = product[k * each : (k + 1) * each].astype(BF16)


def project(groups, paired, text_cache, w_kv):
    depth, features = text_cache.shape
    width = w_kv.shape[1]
    chunks = features // 128
    each = depth // groups
    return pl.pallas_call(
        functools.partial(project_kernel, groups, paired, chunks),
        in_specs=[HBM_SPEC, HBM_SPEC],
        out_specs=[VMEM_SPEC] * groups,
        out_shape=[jax.ShapeDtypeStruct((each, width), BF16)] * groups,
        scratch_shapes=[
            pltpu.VMEM((depth, features), BF16),
            pltpu.VMEM((features, width), BF16),
            pltpu.SemaphoreType.DMA,
            pltpu.SemaphoreType.DMA((chunks,)),
        ],
        compiler_params=kernel_params(),
        name="project",
    )(pltpu.with_memory_space_constraint(text_cache, pltpu.HBM), w_kv)


def select_kernel(groups, each, paired, dp_paired, n_texts, table, *refs):
    texts, pieces, outs, chip_text = refs[:n_texts], refs[n_texts : -2 * groups - 1], refs[-2 * groups - 1 : -1], refs[-1]
    depth = texts[0].shape[0]
    for i, text in enumerate(texts):
        chip_text[i * depth : (i + 1) * depth] = text[...]
    held = jnp.concatenate([piece[...] for piece in pieces], axis=0) if len(pieces) > 1 else pieces[0][...]
    total = held.shape[0]
    index, member = table[3, 0], table[3, 1]
    wanted_rows = groups * SAMPLES * each
    starts, firsts = [], []
    for k in range(groups):
        for s in range(SAMPLES):
            caption = peer(member, k, paired) * SAMPLES + s
            first = first_of_class(table[2, caption], own_residue(member, groups, paired), groups)
            owner = table[1, caption]
            firsts.append(first)
            starts.append((owner ^ index if dp_paired else owner) * each + first)
    shape = (wanted_rows, total)
    target = spread_rows(starts, each, shape)
    inside = spread_rows(firsts, each, shape) < each
    chosen = ((target == lax.broadcasted_iota(jnp.int32, shape, 1)) & inside).astype(BF16)
    rows = jnp.dot(chosen, held, preferred_element_type=F32).astype(BF16)
    size, width = SAMPLES * each, rows.shape[1] // 2
    for k in range(groups):
        outs[k][...] = rows[k * size : (k + 1) * size, :width]
        outs[groups + k][...] = rows[k * size : (k + 1) * size, width:]


def select_rows(groups, each, paired, dp_paired, table, texts, pieces):
    width = pieces[0].shape[1]
    depth, features = texts[0].shape
    return pl.pallas_call(
        functools.partial(select_kernel, groups, each, paired, dp_paired, len(texts)),
        in_specs=[SMEM_SPEC] + [VMEM_SPEC] * (len(texts) + len(pieces)),
        out_specs=[VMEM_SPEC] * (2 * groups + 1),
        out_shape=[jax.ShapeDtypeStruct((SAMPLES * each, width // 2), BF16)] * (2 * groups)
        + [jax.ShapeDtypeStruct((len(texts) * depth, features), BF16)],
        compiler_params=kernel_params(),
        name="select_rows",
    )(table, *texts, *pieces)


LAST = (((1,), (1,)), ((), ()))
FIRST = (((0,), (0,)), ((), ()))


def value_grad_kernel(groups, each, paired, table, queries, cotangent, *refs):
    pieces, (probs, grad_values, scores, probs_rounded) = refs[:groups], refs[groups:]
    tokens, width = queries.shape
    slots = groups * SAMPLES * each
    heads = width // HEAD
    member = table[3, 1]
    split = table[3, 2]
    shape = (slots, tokens)
    rows = lax.broadcasted_iota(jnp.int32, shape, 0)
    position = jnp.zeros(shape, jnp.int32)
    length = jnp.zeros(shape, jnp.int32)
    sample = jnp.zeros(shape, jnp.int32)
    for c in range(groups):
        residue = residue_of(member, c, groups, paired)
        for s in range(SAMPLES):
            caption = member * SAMPLES + s
            run = (c * SAMPLES + s) * each
            here = (rows >= run) & (rows < run + each)
            first = first_of_class(table[2, caption], residue, groups)
            position = jnp.where(here, groups * (first + rows - run) + residue - table[2, caption], position)
            length = jnp.where(here, table[0, caption], length)
            sample = jnp.where(here, s, sample)
    token_sample = (lax.broadcasted_iota(jnp.int32, shape, 1) >= split).astype(jnp.int32)
    allowed = (position < length) & (sample == token_sample)
    for h in range(heads):
        at = slice(h * HEAD, (h + 1) * HEAD)
        k = jnp.concatenate([piece[:, at] for piece in pieces], axis=0)
        scores[h] = lax.dot_general(k, queries[:, at], LAST, preferred_element_type=F32)
    for h in range(heads):
        masked = jnp.where(allowed, scores[h] * HEAD ** (-0.5), F32(-1e30))
        expon = jnp.exp(masked - jnp.max(masked, axis=0, keepdims=True))
        prob = expon / jnp.sum(expon, axis=0, keepdims=True)
        probs[h] = prob
        probs_rounded[h] = prob.astype(BF16)
    for h in range(heads):
        at = slice(h * HEAD, (h + 1) * HEAD)
        grad_values[:, at] = jnp.dot(probs_rounded[h], cotangent[:, at], preferred_element_type=F32).astype(BF16)


def value_grads(groups, each, paired, table, queries, grad_out, pieces):
    tokens, width = queries.shape
    slots = groups * SAMPLES * each
    heads = width // HEAD
    return pl.pallas_call(
        functools.partial(value_grad_kernel, groups, each, paired),
        in_specs=[SMEM_SPEC] + [VMEM_SPEC] * (2 + groups),
        out_specs=[VMEM_SPEC] * 2,
        out_shape=[
            jax.ShapeDtypeStruct((heads, slots, tokens), F32),
            jax.ShapeDtypeStruct((slots, width), BF16),
        ],
        scratch_shapes=[pltpu.VMEM((heads, slots, tokens), F32), pltpu.VMEM((heads, slots, tokens), BF16)],
        compiler_params=kernel_params(),
        name="value_gradients",
    )(table, queries, grad_out, *pieces)


def key_grad_kernel(groups, probs, queries, cotangent, grad_values, *refs):
    values, (score_grads, first_part, last_part, grad_both, prob_grads) = refs[:groups], refs[groups:]
    width = queries.shape[1]
    heads = width // HEAD
    scale = HEAD ** (-0.5)
    for h in range(heads):
        at = slice(h * HEAD, (h + 1) * HEAD)
        v = jnp.concatenate([piece[:, at] for piece in values], axis=0)
        prob_grads[h] = lax.dot_general(v, cotangent[:, at], LAST, preferred_element_type=F32)
    for h in range(heads):
        prob, prob_grad = probs[h], prob_grads[h]
        centre = jnp.sum(prob * prob_grad, axis=0, keepdims=True)
        score_grads[h] = (prob * (prob_grad - centre)).astype(BF16)
    for h in range(heads):
        at = slice(h * HEAD, (h + 1) * HEAD)
        grad_key = jnp.dot(score_grads[h], queries[:, at], preferred_element_type=F32) * scale
        grad_both[:, at] = grad_key.astype(BF16)
    grad_both[:, width:] = grad_values[...]
    cut = first_part.shape[1]
    first_part[...] = grad_both[:, :cut]
    last_part[...] = grad_both[:, cut:]


def key_grads(groups, probs, queries, grad_out, grad_values, values):
    tokens, width = queries.shape
    heads, slots, _ = probs.shape
    return pl.pallas_call(
        functools.partial(key_grad_kernel, groups),
        in_specs=[VMEM_SPEC] * (4 + groups),
        out_specs=[VMEM_SPEC] * 4,
        out_shape=[
            jax.ShapeDtypeStruct((heads, slots, tokens), BF16),
            jax.ShapeDtypeStruct((slots, FIRST_HEADS * HEAD), BF16),
            jax.ShapeDtypeStruct((slots, 2 * width - FIRST_HEADS * HEAD), BF16),
            jax.ShapeDtypeStruct((slots, 2 * width), BF16),
        ],
        scratch_shapes=[pltpu.VMEM((heads, slots, tokens), F32)],
        compiler_params=kernel_params(),
        name="key_gradients",
    )(probs, queries, grad_out, grad_values, *values)


def text_kernel(members, groups, each, depth, paired, dp_paired, table, text, score_grads, *refs):
    keys, (out, grad_query) = refs[:groups], refs[groups:]
    for h in range(score_grads.shape[0]):
        at = slice(h * HEAD, (h + 1) * HEAD)
        k = jnp.concatenate([piece[:, at] for piece in keys], axis=0)
        product = lax.dot_general(score_grads[h], k, FIRST, preferred_element_type=F32)
        grad_query[:, at] = (product * HEAD ** (-0.5)).astype(BF16)
    index, member = table[3, 0], table[3, 1]
    shape = (text.shape[0], out.shape[1])
    columns = lax.broadcasted_iota(jnp.int32, shape, 1)
    runs, place = columns // each, columns % each
    target = jnp.zeros(shape, jnp.int32)
    limit = jnp.zeros(shape, jnp.int32)
    run = 0
    for k in range(members):
        device = peer(member, k, paired)
        for c in range(groups):
            residue = residue_of(device, c, groups, paired)
            for s in range(SAMPLES):
                caption = device * SAMPLES + s
                offset = table[2, caption]
                owner = table[1, caption]
                if dp_paired:
                    owner = owner - (owner & 1) + ((owner ^ index) & 1)
                base = owner * depth
                here = runs == run
                target = jnp.where(here, base + groups * first_of_class(offset, residue, groups) + residue, target)
                limit = jnp.where(here, base + offset + table[0, caption], limit)
                run += 1
    target = target + groups * place
    chosen = ((target == lax.broadcasted_iota(jnp.int32, shape, 0)) & (target < limit)).astype(BF16)
    out[...] = lax.dot_general(text[...], chosen, FIRST, preferred_element_type=F32).astype(BF16)


def slot_texts(members, groups, each, depth, paired, dp_paired, table, text, score_grads, keys):
    features = text.shape[1]
    return pl.pallas_call(
        functools.partial(text_kernel, members, groups, each, depth, paired, dp_paired),
        in_specs=[SMEM_SPEC] + [VMEM_SPEC] * (2 + groups),
        out_specs=[VMEM_SPEC] * 2,
        out_shape=[
            jax.ShapeDtypeStruct((features, members * groups * SAMPLES * each), BF16),
            jax.ShapeDtypeStruct((score_grads.shape[2], keys[0].shape[1]), BF16),
        ],
        compiler_params=kernel_params(),
        name="slot_texts",
    )(table, text, score_grads, *keys)


def weight_kernel(line, start, blocks, *refs):
    chosen_text, *grads = refs[:6] if line else refs[:2]
    out, every, built, sems = refs[-4:]
    at = slice(start, start + every.shape[1])
    if line:
        own, near, inner, second, outer = grads
        member = lax.axis_index("fsdp")
        is_inner = (member == 1) | (member == 2)
        each = own.shape[0]
        every[0:each] = own[:, at]
        every[each : 2 * each] = near[:, at]
        every[2 * each : 3 * each] = second[...]
        every[3 * each :] = jnp.where(is_inner, inner[:, at], outer[...])
    else:
        every[...] = grads[0][:, at]
    rows = built.shape[0] // blocks
    copies = []
    for i in range(blocks):
        block = slice(i * rows, (i + 1) * rows)
        built[block] = jnp.dot(chosen_text[block], every[...], preferred_element_type=F32).astype(BF16)
        copy = pltpu.make_async_copy(
            built.at[pl.ds(i * rows, rows)],
            out.at[pl.ds(i * rows, rows), pl.ds(start, every.shape[1])],
            sems.at[i],
        )
        copy.start()
        copies.append(copy)
    for copy in copies:
        copy.wait()


def weight_grad(line, chosen_text, grads, start, size, before=None):
    features, slots = chosen_text.shape
    width = grads[0].shape[1]
    blocks = 8
    earlier = [] if before is None else [before]
    return pl.pallas_call(
        functools.partial(weight_kernel, line, start, blocks),
        in_specs=[VMEM_SPEC] * (1 + len(grads)) + [ANY_SPEC] * len(earlier),
        out_specs=ANY_SPEC,
        out_shape=jax.ShapeDtypeStruct((features, width), BF16),
        scratch_shapes=[
            pltpu.VMEM((slots, size), BF16),
            pltpu.VMEM((features, size), BF16),
            pltpu.SemaphoreType.DMA((blocks,)),
        ],
        input_output_aliases={1 + len(grads): 0} if earlier else {},
        compiler_params=kernel_params(),
        name="weight_gradient",
    )(chosen_text, *grads, *earlier)


def swap(x, axis, k):
    return lax.ppermute(x, axis, [(i, i ^ k) for i in range(lax.axis_size(axis))])


def gather_dp(x, paired):
    if not paired:
        return [lax.all_gather(x, "dp", axis=0, tiled=True)]
    near = {0: x}
    for k in range(2, lax.axis_size("dp"), 2):
        near[k] = swap(x, "dp", k)
    for k in list(near):
        near[k + 1] = swap(near[k], "dp", 1)
    return [near[k] for k in sorted(near)]


def gather_chips(x):
    size = lax.axis_size("dp")
    cores = [list(range(core, size, 2)) for core in range(2)]
    return lax.all_gather(x, "dp", axis=0, tiled=True, axis_index_groups=cores)


def reduce_line(pieces, members, paired):
    if paired:
        return [pieces[0]] + [swap(pieces[k % len(pieces)], "fsdp", k) for k in range(1, members)]
    return exchange(pieces, paired)


def exchange(pieces, paired):
    if paired:
        return [pieces[0]] + [swap(pieces[k], "fsdp", k) for k in range(1, len(pieces))]
    came = lax.all_to_all(jnp.stack(pieces), "fsdp", 0, 0, tiled=True)
    return [came[k] for k in range(len(pieces))]


def gather_line(parts, both, beside):
    near_pairs = [(0, 1), (1, 0), (2, 3), (3, 2)]
    middle_pairs = [(1, 2), (2, 1)]
    outward = [(1, 0), (2, 3)]
    second = [swap(part, "fsdp", 2) for part in parts]
    near = lax.ppermute(both, "fsdp", near_pairs)
    second[1], beside = lax.optimization_barrier((second[1], beside))
    outer = [lax.ppermute(piece, "fsdp", outward) for piece in second]
    late, _ = lax.optimization_barrier((both, second[1]))
    inner = lax.ppermute(late, "fsdp", middle_pairs)
    return near, inner, second, outer, beside


def shards(
    queries, grad_out, text_cache, w_kv, image_counts, caption_lens, caption_owner, caption_offset
):
    members = lax.axis_size("fsdp")
    line = members == 4
    groups = CLASSES if line else members
    paired = line
    dp_paired = power_of_two(lax.axis_size("dp")) and lax.axis_size("dp") <= 8
    depth = text_cache.shape[0]
    each = depth // groups
    width = queries.shape[1]

    partials = project(groups, paired, text_cache, w_kv)
    partials, late_cache = lax.optimization_barrier((partials, text_cache))
    texts = [late_cache, swap(late_cache, "dp", 1)] if dp_paired else [late_cache]
    came = reduce_line(partials, members, paired)
    table = scalar_table(image_counts, caption_lens, caption_owner, caption_offset)
    rows = sum(piece.astype(F32) for piece in came).astype(BF16)
    class_rows = gather_dp(rows, dp_paired)
    *outgoing, chip_text = select_rows(groups, each, paired, dp_paired, table, texts, class_rows)
    keys = exchange(outgoing[:groups], paired)
    values = exchange(outgoing[groups:], paired)
    probs, grad_values = value_grads(groups, each, paired, table, queries, grad_out, keys)
    grad_values, probs = lax.optimization_barrier((grad_values, probs))
    score_grads, *parts, grad_both = key_grads(groups, probs, queries, grad_out, grad_values, values)
    parts, grad_both, chip_text = lax.optimization_barrier((parts, grad_both, chip_text))
    if dp_paired:
        text = gather_chips(chip_text)
    else:
        text = lax.all_gather(chip_text, "dp", axis=0, tiled=True)
    if line:
        near, inner, second, outer, text = gather_line(parts, grad_both, text)
        operands = [[grad_both, near, inner, second[i], outer[i]] for i in range(2)]
    else:
        operands = [[lax.all_gather(grad_both, "fsdp", axis=0, tiled=True)]] * 2
    chosen_text, grad_query = slot_texts(members, groups, each, depth, paired, dp_paired, table, text, score_grads, keys)
    cut = parts[0].shape[1]
    grad_weight = weight_grad(line, chosen_text, operands[0], 0, cut)
    grad_weight = weight_grad(line, chosen_text, operands[1], cut, 2 * width - cut, grad_weight)
    return grad_query, grad_weight[None]


def solution(mesh):
    in_specs = (
        P(("dp", "fsdp"), None),
        P(("dp", "fsdp"), None),
        P("dp", "fsdp"),
        P("fsdp", None),
        P(("dp", "fsdp"), None),
        P("dp", None),
        P("dp", None),
        P("dp", None),
    )
    out_specs = (P(("dp", "fsdp"), None), P("dp", "fsdp", None))
    return jax.shard_map(shards, mesh=mesh, in_specs=in_specs, out_specs=out_specs, check_vma=False)
```

```python
import functools

import jax
import jax.numpy as jnp
from jax import lax
from jax.experimental import pallas as pl
from jax.experimental.pallas import tpu as pltpu
from jax.sharding import PartitionSpec as P

HEADS = 12
HEAD = 128
LMAX = 32
SAMPLES = 2
FIRST_HEADS = 12
VMEM = 48 * 1024 * 1024

F32 = jnp.float32
BF16 = jnp.bfloat16


def power_of_two(n):
    return n & (n - 1) == 0


def kernel_params(**more):
    return pltpu.CompilerParams(vmem_limit_bytes=VMEM, **more)


SMEM_SPEC = pl.BlockSpec(memory_space=pltpu.SMEM)
VMEM_SPEC = pl.BlockSpec(memory_space=pltpu.VMEM)
ANY_SPEC = pl.BlockSpec(memory_space=pl.ANY)
HBM_SPEC = pl.BlockSpec(memory_space=pltpu.HBM)


def scalar_table(image_counts, caption_lens, caption_owner, caption_offset):
    captions = caption_lens.shape[1]
    place = jnp.stack([lax.axis_index("dp"), lax.axis_index("fsdp"), image_counts[0, 0]]).astype(jnp.int32)
    place = jnp.pad(place, (0, captions - place.shape[0]))
    return jnp.concatenate([caption_lens, caption_owner, caption_offset, place[None]], axis=0)


def peer(index, k, paired):
    return index ^ k if paired else k


def first_of_class(offset, residue, groups):
    return lax.div(offset - residue + groups - 1, jnp.int32(groups))


def spread_rows(values, rows_each, shape):
    rows = lax.broadcasted_iota(jnp.int32, shape, 0)
    result = jnp.zeros(shape, jnp.int32)
    for g, value in enumerate(values):
        result = jnp.where((rows >= g * rows_each) & (rows < (g + 1) * rows_each), value + rows - g * rows_each, result)
    return result


def project_kernel(groups, paired, chunks, cache, weight, *refs):
    outs = refs[:groups]
    held_cache, held_weight, cache_sem, weight_sem = refs[groups:]
    depth = cache.shape[0]
    each = depth // groups
    rows = weight.shape[0] // chunks
    cache_copy = pltpu.make_async_copy(cache, held_cache, cache_sem)
    cache_copy.start()
    copies = [
        pltpu.make_async_copy(weight.at[pl.ds(i * rows, rows)], held_weight.at[pl.ds(i * rows, rows)], weight_sem.at[i])
        for i in range(chunks)
    ]
    for copy in copies:
        copy.start(priority=1)
    member = lax.axis_index("fsdp")
    row = lax.broadcasted_iota(jnp.int32, (depth, depth), 0)
    column = lax.broadcasted_iota(jnp.int32, (depth, depth), 1)
    wanted = jnp.zeros((depth, depth), jnp.int32)
    for k in range(groups):
        residue = peer(member, k, paired)
        wanted = jnp.where(row // each == k, groups * (row - k * each) + residue, wanted)
    order = (wanted == column).astype(BF16)
    cache_copy.wait()
    sorted_rows = jnp.dot(order, held_cache[...], preferred_element_type=F32).astype(BF16)
    product = None
    for i, copy in enumerate(copies):
        copy.wait()
        at = slice(i * rows, (i + 1) * rows)
        part = jnp.dot(sorted_rows[:, at], held_weight[at], preferred_element_type=F32)
        product = part if product is None else product + part
    for k in range(groups):
        outs[k][...] = product[k * each : (k + 1) * each].astype(BF16)


def project(groups, paired, text_cache, w_kv):
    depth, features = text_cache.shape
    width = w_kv.shape[1]
    chunks = features // 128
    each = depth // groups
    return pl.pallas_call(
        functools.partial(project_kernel, groups, paired, chunks),
        in_specs=[HBM_SPEC, HBM_SPEC],
        out_specs=[VMEM_SPEC] * groups,
        out_shape=[jax.ShapeDtypeStruct((each, width), BF16)] * groups,
        scratch_shapes=[
            pltpu.VMEM((depth, features), BF16),
            pltpu.VMEM((features, width), BF16),
            pltpu.SemaphoreType.DMA,
            pltpu.SemaphoreType.DMA((chunks,)),
        ],
        compiler_params=kernel_params(),
        name="project",
    )(pltpu.with_memory_space_constraint(text_cache, pltpu.HBM), w_kv)


def select_kernel(groups, each, paired, dp_paired, n_texts, table, *refs):
    texts, pieces, outs, chip_text = refs[:n_texts], refs[n_texts : -2 * groups - 1], refs[-2 * groups - 1 : -1], refs[-1]
    depth = texts[0].shape[0]
    for i, text in enumerate(texts):
        chip_text[i * depth : (i + 1) * depth] = text[...]
    held = jnp.concatenate([piece[...] for piece in pieces], axis=0) if len(pieces) > 1 else pieces[0][...]
    total = held.shape[0]
    index, member = table[3, 0], table[3, 1]
    wanted_rows = groups * SAMPLES * each
    starts, firsts = [], []
    for k in range(groups):
        for s in range(SAMPLES):
            caption = peer(member, k, paired) * SAMPLES + s
            first = first_of_class(table[2, caption], member, groups)
            owner = table[1, caption]
            firsts.append(first)
            starts.append((owner ^ index if dp_paired else owner) * each + first)
    shape = (wanted_rows, total)
    target = spread_rows(starts, each, shape)
    inside = spread_rows(firsts, each, shape) < each
    chosen = ((target == lax.broadcasted_iota(jnp.int32, shape, 1)) & inside).astype(BF16)
    rows = jnp.dot(chosen, held, preferred_element_type=F32).astype(BF16)
    size, width = SAMPLES * each, rows.shape[1] // 2
    for k in range(groups):
        outs[k][...] = rows[k * size : (k + 1) * size, :width]
        outs[groups + k][...] = rows[k * size : (k + 1) * size, width:]


def select_rows(groups, each, paired, dp_paired, table, texts, pieces):
    width = pieces[0].shape[1]
    depth, features = texts[0].shape
    return pl.pallas_call(
        functools.partial(select_kernel, groups, each, paired, dp_paired, len(texts)),
        in_specs=[SMEM_SPEC] + [VMEM_SPEC] * (len(texts) + len(pieces)),
        out_specs=[VMEM_SPEC] * (2 * groups + 1),
        out_shape=[jax.ShapeDtypeStruct((SAMPLES * each, width // 2), BF16)] * (2 * groups)
        + [jax.ShapeDtypeStruct((len(texts) * depth, features), BF16)],
        compiler_params=kernel_params(),
        name="select_rows",
    )(table, *texts, *pieces)


LAST = (((1,), (1,)), ((), ()))
FIRST = (((0,), (0,)), ((), ()))


def value_grad_kernel(groups, each, paired, table, queries, cotangent, *refs):
    pieces, (probs, grad_values, scores, probs_rounded) = refs[:groups], refs[groups:]
    tokens, width = queries.shape
    slots = groups * SAMPLES * each
    heads = width // HEAD
    member = table[3, 1]
    split = table[3, 2]
    shape = (slots, tokens)
    rows = lax.broadcasted_iota(jnp.int32, shape, 0)
    position = jnp.zeros(shape, jnp.int32)
    length = jnp.zeros(shape, jnp.int32)
    sample = jnp.zeros(shape, jnp.int32)
    for c in range(groups):
        residue = peer(member, c, paired)
        for s in range(SAMPLES):
            caption = member * SAMPLES + s
            run = (c * SAMPLES + s) * each
            here = (rows >= run) & (rows < run + each)
            first = first_of_class(table[2, caption], residue, groups)
            position = jnp.where(here, groups * (first + rows - run) + residue - table[2, caption], position)
            length = jnp.where(here, table[0, caption], length)
            sample = jnp.where(here, s, sample)
    token_sample = (lax.broadcasted_iota(jnp.int32, shape, 1) >= split).astype(jnp.int32)
    allowed = (position < length) & (sample == token_sample)
    for h in range(heads):
        at = slice(h * HEAD, (h + 1) * HEAD)
        k = jnp.concatenate([piece[:, at] for piece in pieces], axis=0)
        scores[h] = lax.dot_general(k, queries[:, at], LAST, preferred_element_type=F32)
    for h in range(heads):
        masked = jnp.where(allowed, scores[h] * HEAD ** (-0.5), F32(-1e30))
        expon = jnp.exp(masked - jnp.max(masked, axis=0, keepdims=True))
        prob = expon / jnp.sum(expon, axis=0, keepdims=True)
        probs[h] = prob
        probs_rounded[h] = prob.astype(BF16)
    for h in range(heads):
        at = slice(h * HEAD, (h + 1) * HEAD)
        grad_values[:, at] = jnp.dot(probs_rounded[h], cotangent[:, at], preferred_element_type=F32).astype(BF16)


def value_grads(groups, each, paired, table, queries, grad_out, pieces):
    tokens, width = queries.shape
    slots = groups * SAMPLES * each
    heads = width // HEAD
    return pl.pallas_call(
        functools.partial(value_grad_kernel, groups, each, paired),
        in_specs=[SMEM_SPEC] + [VMEM_SPEC] * (2 + groups),
        out_specs=[VMEM_SPEC] * 2,
        out_shape=[
            jax.ShapeDtypeStruct((heads, slots, tokens), F32),
            jax.ShapeDtypeStruct((slots, width), BF16),
        ],
        scratch_shapes=[pltpu.VMEM((heads, slots, tokens), F32), pltpu.VMEM((heads, slots, tokens), BF16)],
        compiler_params=kernel_params(),
        name="value_gradients",
    )(table, queries, grad_out, *pieces)


def key_grad_kernel(groups, probs, queries, cotangent, grad_values, *refs):
    values, (score_grads, first_part, last_part, grad_both, prob_grads) = refs[:groups], refs[groups:]
    width = queries.shape[1]
    heads = width // HEAD
    scale = HEAD ** (-0.5)
    for h in range(heads):
        at = slice(h * HEAD, (h + 1) * HEAD)
        v = jnp.concatenate([piece[:, at] for piece in values], axis=0)
        prob_grads[h] = lax.dot_general(v, cotangent[:, at], LAST, preferred_element_type=F32)
    for h in range(heads):
        prob, prob_grad = probs[h], prob_grads[h]
        centre = jnp.sum(prob * prob_grad, axis=0, keepdims=True)
        score_grads[h] = (prob * (prob_grad - centre)).astype(BF16)
    for h in range(heads):
        at = slice(h * HEAD, (h + 1) * HEAD)
        grad_key = jnp.dot(score_grads[h], queries[:, at], preferred_element_type=F32) * scale
        grad_both[:, at] = grad_key.astype(BF16)
    grad_both[:, width:] = grad_values[...]
    cut = first_part.shape[1]
    first_part[...] = grad_both[:, :cut]
    last_part[...] = grad_both[:, cut:]


def key_grads(groups, probs, queries, grad_out, grad_values, values):
    tokens, width = queries.shape
    heads, slots, _ = probs.shape
    return pl.pallas_call(
        functools.partial(key_grad_kernel, groups),
        in_specs=[VMEM_SPEC] * (4 + groups),
        out_specs=[VMEM_SPEC] * 4,
        out_shape=[
            jax.ShapeDtypeStruct((heads, slots, tokens), BF16),
            jax.ShapeDtypeStruct((slots, FIRST_HEADS * HEAD), BF16),
            jax.ShapeDtypeStruct((slots, 2 * width - FIRST_HEADS * HEAD), BF16),
            jax.ShapeDtypeStruct((slots, 2 * width), BF16),
        ],
        scratch_shapes=[pltpu.VMEM((heads, slots, tokens), F32)],
        compiler_params=kernel_params(),
        name="key_gradients",
    )(probs, queries, grad_out, grad_values, *values)


def text_kernel(members, groups, each, depth, paired, dp_paired, table, text, score_grads, *refs):
    keys, (out, grad_query) = refs[:groups], refs[groups:]
    for h in range(score_grads.shape[0]):
        at = slice(h * HEAD, (h + 1) * HEAD)
        k = jnp.concatenate([piece[:, at] for piece in keys], axis=0)
        product = lax.dot_general(score_grads[h], k, FIRST, preferred_element_type=F32)
        grad_query[:, at] = (product * HEAD ** (-0.5)).astype(BF16)
    index, member = table[3, 0], table[3, 1]
    shape = (text.shape[0], out.shape[1])
    columns = lax.broadcasted_iota(jnp.int32, shape, 1)
    runs, place = columns // each, columns % each
    target = jnp.zeros(shape, jnp.int32)
    limit = jnp.zeros(shape, jnp.int32)
    run = 0
    for k in range(members):
        device = peer(member, k, paired)
        for c in range(groups):
            residue = peer(device, c, paired)
            for s in range(SAMPLES):
                caption = device * SAMPLES + s
                offset = table[2, caption]
                owner = table[1, caption]
                if dp_paired:
                    owner = owner - (owner & 1) + ((owner ^ index) & 1)
                base = owner * depth
                here = runs == run
                target = jnp.where(here, base + groups * first_of_class(offset, residue, groups) + residue, target)
                limit = jnp.where(here, base + offset + table[0, caption], limit)
                run += 1
    target = target + groups * place
    chosen = ((target == lax.broadcasted_iota(jnp.int32, shape, 0)) & (target < limit)).astype(BF16)
    out[...] = lax.dot_general(text[...], chosen, FIRST, preferred_element_type=F32).astype(BF16)


def slot_texts(members, groups, each, depth, paired, dp_paired, table, text, score_grads, keys):
    features = text.shape[1]
    return pl.pallas_call(
        functools.partial(text_kernel, members, groups, each, depth, paired, dp_paired),
        in_specs=[SMEM_SPEC] + [VMEM_SPEC] * (2 + groups),
        out_specs=[VMEM_SPEC] * 2,
        out_shape=[
            jax.ShapeDtypeStruct((features, members * groups * SAMPLES * each), BF16),
            jax.ShapeDtypeStruct((score_grads.shape[2], keys[0].shape[1]), BF16),
        ],
        compiler_params=kernel_params(),
        name="slot_texts",
    )(table, text, score_grads, *keys)


def weight_kernel(line, start, blocks, *refs):
    chosen_text, *grads = refs[:6] if line else refs[:2]
    out, every, built, sems = refs[-4:]
    at = slice(start, start + every.shape[1])
    if line:
        own, near, inner, second, outer = grads
        member = lax.axis_index("fsdp")
        is_inner = (member == 1) | (member == 2)
        each = own.shape[0]
        every[0:each] = own[:, at]
        every[each : 2 * each] = near[:, at]
        every[2 * each : 3 * each] = second[...]
        every[3 * each :] = jnp.where(is_inner, inner[:, at], outer[...])
    else:
        every[...] = grads[0][:, at]
    rows = built.shape[0] // blocks
    copies = []
    for i in range(blocks):
        block = slice(i * rows, (i + 1) * rows)
        built[block] = jnp.dot(chosen_text[block], every[...], preferred_element_type=F32).astype(BF16)
        copy = pltpu.make_async_copy(
            built.at[pl.ds(i * rows, rows)],
            out.at[pl.ds(i * rows, rows), pl.ds(start, every.shape[1])],
            sems.at[i],
        )
        copy.start()
        copies.append(copy)
    for copy in copies:
        copy.wait()


def weight_grad(line, chosen_text, grads, start, size, before=None):
    features, slots = chosen_text.shape
    width = grads[0].shape[1]
    blocks = 8
    earlier = [] if before is None else [before]
    return pl.pallas_call(
        functools.partial(weight_kernel, line, start, blocks),
        in_specs=[VMEM_SPEC] * (1 + len(grads)) + [ANY_SPEC] * len(earlier),
        out_specs=ANY_SPEC,
        out_shape=jax.ShapeDtypeStruct((features, width), BF16),
        scratch_shapes=[
            pltpu.VMEM((slots, size), BF16),
            pltpu.VMEM((features, size), BF16),
            pltpu.SemaphoreType.DMA((blocks,)),
        ],
        input_output_aliases={1 + len(grads): 0} if earlier else {},
        compiler_params=kernel_params(),
        name="weight_gradient",
    )(chosen_text, *grads, *earlier)


def swap(x, axis, k):
    return lax.ppermute(x, axis, [(i, i ^ k) for i in range(lax.axis_size(axis))])


def gather_dp(x, paired):
    if not paired:
        return [lax.all_gather(x, "dp", axis=0, tiled=True)]
    near = {0: x}
    for k in range(2, lax.axis_size("dp"), 2):
        near[k] = swap(x, "dp", k)
    for k in list(near):
        near[k + 1] = swap(near[k], "dp", 1)
    return [near[k] for k in sorted(near)]


def gather_chips(x):
    size = lax.axis_size("dp")
    cores = [list(range(core, size, 2)) for core in range(2)]
    return lax.all_gather(x, "dp", axis=0, tiled=True, axis_index_groups=cores)


def reduce_line(pieces, members, paired):
    if paired:
        distances = sorted(range(1, members), key=lambda k: (k != 2, k))
        return [pieces[0]] + [swap(pieces[k], "fsdp", k) for k in distances]
    return exchange(pieces, paired)


def exchange(pieces, paired):
    if paired:
        return [pieces[0]] + [swap(pieces[k], "fsdp", k) for k in range(1, len(pieces))]
    came = lax.all_to_all(jnp.stack(pieces), "fsdp", 0, 0, tiled=True)
    return [came[k] for k in range(len(pieces))]


def gather_line(parts, both, beside):
    near_pairs = [(0, 1), (1, 0), (2, 3), (3, 2)]
    middle_pairs = [(1, 2), (2, 1)]
    outward = [(1, 0), (2, 3)]
    second = [swap(part, "fsdp", 2) for part in parts]
    near = lax.ppermute(both, "fsdp", near_pairs)
    second[1], beside = lax.optimization_barrier((second[1], beside))
    outer = [lax.ppermute(piece, "fsdp", outward) for piece in second]
    late, _ = lax.optimization_barrier((both, second[1]))
    inner = lax.ppermute(late, "fsdp", middle_pairs)
    return near, inner, second, outer, beside


def shards(
    queries, grad_out, text_cache, w_kv, image_counts, caption_lens, caption_owner, caption_offset
):
    members = lax.axis_size("fsdp")
    line = members == 4
    groups = members
    paired = line
    dp_paired = power_of_two(lax.axis_size("dp")) and lax.axis_size("dp") <= 8
    depth = text_cache.shape[0]
    each = depth // groups
    width = queries.shape[1]

    partials = project(groups, paired, text_cache, w_kv)
    partials, late_cache = lax.optimization_barrier((partials, text_cache))
    texts = [late_cache, swap(late_cache, "dp", 1)] if dp_paired else [late_cache]
    came = reduce_line(partials, members, paired)
    table = scalar_table(image_counts, caption_lens, caption_owner, caption_offset)
    rows = sum(piece.astype(F32) for piece in came).astype(BF16)
    class_rows = gather_dp(rows, dp_paired)
    *outgoing, chip_text = select_rows(groups, each, paired, dp_paired, table, texts, class_rows)
    keys = exchange(outgoing[:groups], paired)
    values = exchange(outgoing[groups:], paired)
    probs, grad_values = value_grads(groups, each, paired, table, queries, grad_out, keys)
    grad_values, probs = lax.optimization_barrier((grad_values, probs))
    score_grads, *parts, grad_both = key_grads(groups, probs, queries, grad_out, grad_values, values)
    parts, grad_both, chip_text = lax.optimization_barrier((parts, grad_both, chip_text))
    if dp_paired:
        text = gather_chips(chip_text)
    else:
        text = lax.all_gather(chip_text, "dp", axis=0, tiled=True)
    if line:
        near, inner, second, outer, text = gather_line(parts, grad_both, text)
        operands = [[grad_both, near, inner, second[i], outer[i]] for i in range(2)]
    else:
        operands = [[lax.all_gather(grad_both, "fsdp", axis=0, tiled=True)]] * 2
    chosen_text, grad_query = slot_texts(members, groups, each, depth, paired, dp_paired, table, text, score_grads, keys)
    cut = parts[0].shape[1]
    grad_weight = weight_grad(line, chosen_text, operands[0], 0, cut)
    grad_weight = weight_grad(line, chosen_text, operands[1], cut, 2 * width - cut, grad_weight)
    return grad_query, grad_weight[None]


def solution(mesh):
    in_specs = (
        P(("dp", "fsdp"), None),
        P(("dp", "fsdp"), None),
        P("dp", "fsdp"),
        P("fsdp", None),
        P(("dp", "fsdp"), None),
        P("dp", None),
        P("dp", None),
        P("dp", None),
    )
    out_specs = (P(("dp", "fsdp"), None), P("dp", "fsdp", None))
    return jax.shard_map(shards, mesh=mesh, in_specs=in_specs, out_specs=out_specs, check_vma=False)
```

```python
import functools

import jax
import jax.numpy as jnp
from jax import lax
from jax.experimental import pallas as pl
from jax.experimental.pallas import tpu as pltpu
from jax.sharding import PartitionSpec as P

HEADS = 12
HEAD = 128
LMAX = 32
SAMPLES = 2
FIRST_HEADS = 12
VMEM = 48 * 1024 * 1024

F32 = jnp.float32
BF16 = jnp.bfloat16


def power_of_two(n):
    return n & (n - 1) == 0


def kernel_params(**more):
    return pltpu.CompilerParams(vmem_limit_bytes=VMEM, **more)


SMEM_SPEC = pl.BlockSpec(memory_space=pltpu.SMEM)
VMEM_SPEC = pl.BlockSpec(memory_space=pltpu.VMEM)
ANY_SPEC = pl.BlockSpec(memory_space=pl.ANY)
HBM_SPEC = pl.BlockSpec(memory_space=pltpu.HBM)


def scalar_table(image_counts, caption_lens, caption_owner, caption_offset):
    captions = caption_lens.shape[1]
    place = jnp.stack([lax.axis_index("dp"), lax.axis_index("fsdp"), image_counts[0, 0]]).astype(jnp.int32)
    place = jnp.pad(place, (0, captions - place.shape[0]))
    return jnp.concatenate([caption_lens, caption_owner, caption_offset, place[None]], axis=0)


def peer(index, k, paired):
    return index ^ k if paired else k


def first_of_class(offset, residue, groups):
    return lax.div(offset - residue + groups - 1, jnp.int32(groups))


def spread_rows(values, rows_each, shape):
    rows = lax.broadcasted_iota(jnp.int32, shape, 0)
    result = jnp.zeros(shape, jnp.int32)
    for g, value in enumerate(values):
        result = jnp.where((rows >= g * rows_each) & (rows < (g + 1) * rows_each), value + rows - g * rows_each, result)
    return result


def project_kernel(groups, paired, chunks, cache, weight, *refs):
    outs = refs[:groups]
    held_cache, held_weight, cache_sem, weight_sem = refs[groups:]
    depth = cache.shape[0]
    each = depth // groups
    rows = weight.shape[0] // chunks
    cache_copy = pltpu.make_async_copy(cache, held_cache, cache_sem)
    cache_copy.start()
    copies = [
        pltpu.make_async_copy(weight.at[pl.ds(i * rows, rows)], held_weight.at[pl.ds(i * rows, rows)], weight_sem.at[i])
        for i in range(chunks)
    ]
    for copy in copies:
        copy.start(priority=1)
    member = lax.axis_index("fsdp")
    row = lax.broadcasted_iota(jnp.int32, (depth, depth), 0)
    column = lax.broadcasted_iota(jnp.int32, (depth, depth), 1)
    wanted = jnp.zeros((depth, depth), jnp.int32)
    for k in range(groups):
        residue = peer(member, k, paired)
        wanted = jnp.where(row // each == k, groups * (row - k * each) + residue, wanted)
    order = (wanted == column).astype(BF16)
    cache_copy.wait()
    sorted_rows = jnp.dot(order, held_cache[...], preferred_element_type=F32).astype(BF16)
    product = None
    for i, copy in enumerate(copies):
        copy.wait()
        at = slice(i * rows, (i + 1) * rows)
        part = jnp.dot(sorted_rows[:, at], held_weight[at], preferred_element_type=F32)
        product = part if product is None else product + part
    for k in range(groups):
        outs[k][...] = product[k * each : (k + 1) * each].astype(BF16)


def project(groups, paired, text_cache, w_kv):
    depth, features = text_cache.shape
    width = w_kv.shape[1]
    chunks = features // 128
    each = depth // groups
    return pl.pallas_call(
        functools.partial(project_kernel, groups, paired, chunks),
        in_specs=[HBM_SPEC, HBM_SPEC],
        out_specs=[VMEM_SPEC] * groups,
        out_shape=[jax.ShapeDtypeStruct((each, width), BF16)] * groups,
        scratch_shapes=[
            pltpu.VMEM((depth, features), BF16),
            pltpu.VMEM((features, width), BF16),
            pltpu.SemaphoreType.DMA,
            pltpu.SemaphoreType.DMA((chunks,)),
        ],
        compiler_params=kernel_params(),
        name="project",
    )(pltpu.with_memory_space_constraint(text_cache, pltpu.HBM), w_kv)


def select_kernel(groups, each, paired, dp_paired, n_texts, table, *refs):
    texts, pieces, outs, chip_text = refs[:n_texts], refs[n_texts : -2 * groups - 1], refs[-2 * groups - 1 : -1], refs[-1]
    depth = texts[0].shape[0]
    for i, text in enumerate(texts):
        chip_text[i * depth : (i + 1) * depth] = text[...]
    held = jnp.concatenate([piece[...] for piece in pieces], axis=0) if len(pieces) > 1 else pieces[0][...]
    total = held.shape[0]
    index, member = table[3, 0], table[3, 1]
    wanted_rows = groups * SAMPLES * each
    starts, firsts = [], []
    for k in range(groups):
        for s in range(SAMPLES):
            caption = peer(member, k, paired) * SAMPLES + s
            first = first_of_class(table[2, caption], member, groups)
            owner = table[1, caption]
            firsts.append(first)
            starts.append((owner ^ index if dp_paired else owner) * each + first)
    shape = (wanted_rows, total)
    target = spread_rows(starts, each, shape)
    inside = spread_rows(firsts, each, shape) < each
    chosen = ((target == lax.broadcasted_iota(jnp.int32, shape, 1)) & inside).astype(BF16)
    rows = jnp.dot(chosen, held, preferred_element_type=F32).astype(BF16)
    size, width = SAMPLES * each, rows.shape[1] // 2
    for k in range(groups):
        outs[k][...] = rows[k * size : (k + 1) * size, :width]
        outs[groups + k][...] = rows[k * size : (k + 1) * size, width:]


def select_rows(groups, each, paired, dp_paired, table, texts, pieces):
    width = pieces[0].shape[1]
    depth, features = texts[0].shape
    return pl.pallas_call(
        functools.partial(select_kernel, groups, each, paired, dp_paired, len(texts)),
        in_specs=[SMEM_SPEC] + [VMEM_SPEC] * (len(texts) + len(pieces)),
        out_specs=[VMEM_SPEC] * (2 * groups + 1),
        out_shape=[jax.ShapeDtypeStruct((SAMPLES * each, width // 2), BF16)] * (2 * groups)
        + [jax.ShapeDtypeStruct((len(texts) * depth, features), BF16)],
        compiler_params=kernel_params(),
        name="select_rows",
    )(table, *texts, *pieces)


LAST = (((1,), (1,)), ((), ()))
FIRST = (((0,), (0,)), ((), ()))


def value_grad_kernel(groups, each, paired, table, queries, cotangent, *refs):
    pieces, (probs, grad_values, scores, probs_rounded) = refs[:groups], refs[groups:]
    tokens, width = queries.shape
    slots = groups * SAMPLES * each
    heads = width // HEAD
    member = table[3, 1]
    split = table[3, 2]
    shape = (slots, tokens)
    rows = lax.broadcasted_iota(jnp.int32, shape, 0)
    position = jnp.zeros(shape, jnp.int32)
    length = jnp.zeros(shape, jnp.int32)
    sample = jnp.zeros(shape, jnp.int32)
    for c in range(groups):
        residue = peer(member, c, paired)
        for s in range(SAMPLES):
            caption = member * SAMPLES + s
            run = (c * SAMPLES + s) * each
            here = (rows >= run) & (rows < run + each)
            first = first_of_class(table[2, caption], residue, groups)
            position = jnp.where(here, groups * (first + rows - run) + residue - table[2, caption], position)
            length = jnp.where(here, table[0, caption], length)
            sample = jnp.where(here, s, sample)
    token_sample = (lax.broadcasted_iota(jnp.int32, shape, 1) >= split).astype(jnp.int32)
    allowed = (position < length) & (sample == token_sample)
    for h in range(heads):
        at = slice(h * HEAD, (h + 1) * HEAD)
        k = jnp.concatenate([piece[:, at] for piece in pieces], axis=0)
        scores[h] = lax.dot_general(k, queries[:, at], LAST, preferred_element_type=F32)
    for h in range(heads):
        masked = jnp.where(allowed, scores[h] * HEAD ** (-0.5), F32(-1e30))
        expon = jnp.exp(masked - jnp.max(masked, axis=0, keepdims=True))
        prob = expon / jnp.sum(expon, axis=0, keepdims=True)
        probs[h] = prob
        probs_rounded[h] = prob.astype(BF16)
    for h in range(heads):
        at = slice(h * HEAD, (h + 1) * HEAD)
        grad_values[:, at] = jnp.dot(probs_rounded[h], cotangent[:, at], preferred_element_type=F32).astype(BF16)


def value_grads(groups, each, paired, table, queries, grad_out, pieces):
    tokens, width = queries.shape
    slots = groups * SAMPLES * each
    heads = width // HEAD
    return pl.pallas_call(
        functools.partial(value_grad_kernel, groups, each, paired),
        in_specs=[SMEM_SPEC] + [VMEM_SPEC] * (2 + groups),
        out_specs=[VMEM_SPEC] * 2,
        out_shape=[
            jax.ShapeDtypeStruct((heads, slots, tokens), F32),
            jax.ShapeDtypeStruct((slots, width), BF16),
        ],
        scratch_shapes=[pltpu.VMEM((heads, slots, tokens), F32), pltpu.VMEM((heads, slots, tokens), BF16)],
        compiler_params=kernel_params(),
        name="value_gradients",
    )(table, queries, grad_out, *pieces)


def key_grad_kernel(groups, probs, queries, cotangent, grad_values, *refs):
    values, (score_grads, first_part, last_part, grad_both, prob_grads) = refs[:groups], refs[groups:]
    width = queries.shape[1]
    heads = width // HEAD
    scale = HEAD ** (-0.5)
    for h in range(heads):
        at = slice(h * HEAD, (h + 1) * HEAD)
        v = jnp.concatenate([piece[:, at] for piece in values], axis=0)
        prob_grads[h] = lax.dot_general(v, cotangent[:, at], LAST, preferred_element_type=F32)
    for h in range(heads):
        prob, prob_grad = probs[h], prob_grads[h]
        centre = jnp.sum(prob * prob_grad, axis=0, keepdims=True)
        score_grads[h] = (prob * (prob_grad - centre)).astype(BF16)
    for h in range(heads):
        at = slice(h * HEAD, (h + 1) * HEAD)
        grad_key = jnp.dot(score_grads[h], queries[:, at], preferred_element_type=F32) * scale
        grad_both[:, at] = grad_key.astype(BF16)
    grad_both[:, width:] = grad_values[...]
    cut = first_part.shape[1]
    first_part[...] = grad_both[:, :cut]
    last_part[...] = grad_both[:, cut:]


def key_grads(groups, probs, queries, grad_out, grad_values, values):
    tokens, width = queries.shape
    heads, slots, _ = probs.shape
    return pl.pallas_call(
        functools.partial(key_grad_kernel, groups),
        in_specs=[VMEM_SPEC] * (4 + groups),
        out_specs=[VMEM_SPEC] * 4,
        out_shape=[
            jax.ShapeDtypeStruct((heads, slots, tokens), BF16),
            jax.ShapeDtypeStruct((slots, FIRST_HEADS * HEAD), BF16),
            jax.ShapeDtypeStruct((slots, 2 * width - FIRST_HEADS * HEAD), BF16),
            jax.ShapeDtypeStruct((slots, 2 * width), BF16),
        ],
        scratch_shapes=[pltpu.VMEM((heads, slots, tokens), F32)],
        compiler_params=kernel_params(),
        name="key_gradients",
    )(probs, queries, grad_out, grad_values, *values)


def text_kernel(members, groups, each, depth, paired, dp_paired, table, text, score_grads, *refs):
    keys, (out, grad_query) = refs[:groups], refs[groups:]
    for h in range(score_grads.shape[0]):
        at = slice(h * HEAD, (h + 1) * HEAD)
        k = jnp.concatenate([piece[:, at] for piece in keys], axis=0)
        product = lax.dot_general(score_grads[h], k, FIRST, preferred_element_type=F32)
        grad_query[:, at] = (product * HEAD ** (-0.5)).astype(BF16)
    index, member = table[3, 0], table[3, 1]
    shape = (text.shape[0], out.shape[1])
    columns = lax.broadcasted_iota(jnp.int32, shape, 1)
    runs, place = columns // each, columns % each
    target = jnp.zeros(shape, jnp.int32)
    limit = jnp.zeros(shape, jnp.int32)
    run = 0
    for k in range(members):
        device = peer(member, k, paired)
        for c in range(groups):
            residue = peer(device, c, paired)
            for s in range(SAMPLES):
                caption = device * SAMPLES + s
                offset = table[2, caption]
                owner = table[1, caption]
                if dp_paired:
                    owner = owner - (owner & 1) + ((owner ^ index) & 1)
                base = owner * depth
                here = runs == run
                target = jnp.where(here, base + groups * first_of_class(offset, residue, groups) + residue, target)
                limit = jnp.where(here, base + offset + table[0, caption], limit)
                run += 1
    target = target + groups * place
    chosen = ((target == lax.broadcasted_iota(jnp.int32, shape, 0)) & (target < limit)).astype(BF16)
    out[...] = lax.dot_general(text[...], chosen, FIRST, preferred_element_type=F32).astype(BF16)


def slot_texts(members, groups, each, depth, paired, dp_paired, table, text, score_grads, keys):
    features = text.shape[1]
    return pl.pallas_call(
        functools.partial(text_kernel, members, groups, each, depth, paired, dp_paired),
        in_specs=[SMEM_SPEC] + [VMEM_SPEC] * (2 + groups),
        out_specs=[VMEM_SPEC] * 2,
        out_shape=[
            jax.ShapeDtypeStruct((features, members * groups * SAMPLES * each), BF16),
            jax.ShapeDtypeStruct((score_grads.shape[2], keys[0].shape[1]), BF16),
        ],
        compiler_params=kernel_params(),
        name="slot_texts",
    )(table, text, score_grads, *keys)


def weight_kernel(line, start, blocks, *refs):
    chosen_text, *grads = refs[:6] if line else refs[:2]
    out, every, built, sems = refs[-4:]
    at = slice(start, start + every.shape[1])
    if line:
        own, near, inner, second, outer = grads
        member = lax.axis_index("fsdp")
        is_inner = (member == 1) | (member == 2)
        each = own.shape[0]
        every[0:each] = own[:, at]
        every[each : 2 * each] = near[:, at]
        every[2 * each : 3 * each] = second[...]
        every[3 * each :] = jnp.where(is_inner, inner[:, at], outer[...])
    else:
        every[...] = grads[0][:, at]
    rows = built.shape[0] // blocks
    copies = []
    for i in range(blocks):
        block = slice(i * rows, (i + 1) * rows)
        built[block] = jnp.dot(chosen_text[block], every[...], preferred_element_type=F32).astype(BF16)
        copy = pltpu.make_async_copy(
            built.at[pl.ds(i * rows, rows)],
            out.at[pl.ds(i * rows, rows), pl.ds(start, every.shape[1])],
            sems.at[i],
        )
        copy.start()
        copies.append(copy)
    for copy in copies:
        copy.wait()


def weight_grad(line, chosen_text, grads, start, size, before=None):
    features, slots = chosen_text.shape
    width = grads[0].shape[1]
    blocks = 8
    earlier = [] if before is None else [before]
    return pl.pallas_call(
        functools.partial(weight_kernel, line, start, blocks),
        in_specs=[VMEM_SPEC] * (1 + len(grads)) + [ANY_SPEC] * len(earlier),
        out_specs=ANY_SPEC,
        out_shape=jax.ShapeDtypeStruct((features, width), BF16),
        scratch_shapes=[
            pltpu.VMEM((slots, size), BF16),
            pltpu.VMEM((features, size), BF16),
            pltpu.SemaphoreType.DMA((blocks,)),
        ],
        input_output_aliases={1 + len(grads): 0} if earlier else {},
        compiler_params=kernel_params(),
        name="weight_gradient",
    )(chosen_text, *grads, *earlier)


def swap(x, axis, k):
    return lax.ppermute(x, axis, [(i, i ^ k) for i in range(lax.axis_size(axis))])


def gather_dp(x, paired):
    if not paired:
        return [lax.all_gather(x, "dp", axis=0, tiled=True)]
    near = {0: x}
    for k in range(2, lax.axis_size("dp"), 2):
        near[k] = swap(x, "dp", k)
    for k in list(near):
        near[k + 1] = swap(near[k], "dp", 1)
    return [near[k] for k in sorted(near)]


def gather_chips(x):
    size = lax.axis_size("dp")
    cores = [list(range(core, size, 2)) for core in range(2)]
    return lax.all_gather(x, "dp", axis=0, tiled=True, axis_index_groups=cores)


def reduce_line(pieces, members, paired):
    if paired:
        distances = sorted(range(1, members), key=lambda k: (k != 2, k))
        return [pieces[0]] + [swap(pieces[k], "fsdp", k) for k in distances]
    return exchange(pieces, paired)


def exchange(pieces, paired):
    if paired:
        return [pieces[0]] + [swap(pieces[k], "fsdp", k) for k in range(1, len(pieces))]
    came = lax.all_to_all(jnp.stack(pieces), "fsdp", 0, 0, tiled=True)
    return [came[k] for k in range(len(pieces))]


def gather_line(parts, both, beside):
    near_pairs = [(0, 1), (1, 0), (2, 3), (3, 2)]
    middle_pairs = [(1, 2), (2, 1)]
    outward = [(1, 0), (2, 3)]
    second = [swap(part, "fsdp", 2) for part in parts]
    near = lax.ppermute(both, "fsdp", near_pairs)
    second[0], beside = lax.optimization_barrier((second[0], beside))
    outer = [lax.ppermute(piece, "fsdp", outward) for piece in second]
    late, _ = lax.optimization_barrier((both, second[0]))
    inner = lax.ppermute(late, "fsdp", middle_pairs)
    return near, inner, second, outer, beside


def shards(
    queries, grad_out, text_cache, w_kv, image_counts, caption_lens, caption_owner, caption_offset
):
    members = lax.axis_size("fsdp")
    line = members == 4
    groups = members
    paired = line
    dp_paired = power_of_two(lax.axis_size("dp")) and lax.axis_size("dp") <= 8
    depth = text_cache.shape[0]
    each = depth // groups
    width = queries.shape[1]

    partials = project(groups, paired, text_cache, w_kv)
    partials, late_cache = lax.optimization_barrier((partials, text_cache))
    texts = [late_cache, swap(late_cache, "dp", 1)] if dp_paired else [late_cache]
    came = reduce_line(partials, members, paired)
    table = scalar_table(image_counts, caption_lens, caption_owner, caption_offset)
    rows = sum(piece.astype(F32) for piece in came).astype(BF16)
    class_rows = gather_dp(rows, dp_paired)
    *outgoing, chip_text = select_rows(groups, each, paired, dp_paired, table, texts, class_rows)
    keys = exchange(outgoing[:groups], paired)
    values = exchange(outgoing[groups:], paired)
    probs, grad_values = value_grads(groups, each, paired, table, queries, grad_out, keys)
    grad_values, probs = lax.optimization_barrier((grad_values, probs))
    score_grads, *parts, grad_both = key_grads(groups, probs, queries, grad_out, grad_values, values)
    parts, grad_both, chip_text = lax.optimization_barrier((parts, grad_both, chip_text))
    if dp_paired:
        text = gather_chips(chip_text)
    else:
        text = lax.all_gather(chip_text, "dp", axis=0, tiled=True)
    if line:
        near, inner, second, outer, text = gather_line(parts, grad_both, text)
        operands = [[grad_both, near, inner, second[i], outer[i]] for i in range(2)]
    else:
        operands = [[lax.all_gather(grad_both, "fsdp", axis=0, tiled=True)]] * 2
    chosen_text, grad_query = slot_texts(members, groups, each, depth, paired, dp_paired, table, text, score_grads, keys)
    cut = parts[0].shape[1]
    grad_weight = weight_grad(line, chosen_text, operands[1], cut, 2 * width - cut)
    grad_weight = weight_grad(line, chosen_text, operands[0], 0, cut, grad_weight)
    return grad_query, grad_weight[None]


def solution(mesh):
    in_specs = (
        P(("dp", "fsdp"), None),
        P(("dp", "fsdp"), None),
        P("dp", "fsdp"),
        P("fsdp", None),
        P(("dp", "fsdp"), None),
        P("dp", None),
        P("dp", None),
        P("dp", None),
    )
    out_specs = (P(("dp", "fsdp"), None), P("dp", "fsdp", None))
    return jax.shard_map(shards, mesh=mesh, in_specs=in_specs, out_specs=out_specs, check_vma=False)
```

```python
import functools

import jax
import jax.numpy as jnp
from jax import lax
from jax.experimental import pallas as pl
from jax.experimental.pallas import tpu as pltpu
from jax.sharding import PartitionSpec as P

HEADS = 12
HEAD = 128
LMAX = 32
SAMPLES = 2
FIRST_HEADS = 12
VMEM = 48 * 1024 * 1024

F32 = jnp.float32
BF16 = jnp.bfloat16


def power_of_two(n):
    return n & (n - 1) == 0


def kernel_params(**more):
    return pltpu.CompilerParams(vmem_limit_bytes=VMEM, **more)


SMEM_SPEC = pl.BlockSpec(memory_space=pltpu.SMEM)
VMEM_SPEC = pl.BlockSpec(memory_space=pltpu.VMEM)
ANY_SPEC = pl.BlockSpec(memory_space=pl.ANY)
HBM_SPEC = pl.BlockSpec(memory_space=pltpu.HBM)


def scalar_table(image_counts, caption_lens, caption_owner, caption_offset):
    captions = caption_lens.shape[1]
    place = jnp.stack([lax.axis_index("dp"), lax.axis_index("fsdp"), image_counts[0, 0]]).astype(jnp.int32)
    place = jnp.pad(place, (0, captions - place.shape[0]))
    return jnp.concatenate([caption_lens, caption_owner, caption_offset, place[None]], axis=0)


def peer(index, k, paired):
    return index ^ k if paired else k


def first_of_class(offset, residue, groups):
    return lax.div(offset - residue + groups - 1, jnp.int32(groups))


def spread_rows(values, rows_each, shape):
    rows = lax.broadcasted_iota(jnp.int32, shape, 0)
    result = jnp.zeros(shape, jnp.int32)
    for g, value in enumerate(values):
        result = jnp.where((rows >= g * rows_each) & (rows < (g + 1) * rows_each), value + rows - g * rows_each, result)
    return result


def project_kernel(groups, paired, chunks, cache, weight, *refs):
    outs = refs[:groups]
    held_cache, held_weight, cache_sem, weight_sem = refs[groups:]
    depth = cache.shape[0]
    each = depth // groups
    rows = weight.shape[0] // chunks
    cache_copy = pltpu.make_async_copy(cache, held_cache, cache_sem)
    cache_copy.start()
    copies = [
        pltpu.make_async_copy(weight.at[pl.ds(i * rows, rows)], held_weight.at[pl.ds(i * rows, rows)], weight_sem.at[i])
        for i in range(chunks)
    ]
    for copy in copies:
        copy.start(priority=1)
    member = lax.axis_index("fsdp")
    row = lax.broadcasted_iota(jnp.int32, (depth, depth), 0)
    column = lax.broadcasted_iota(jnp.int32, (depth, depth), 1)
    wanted = jnp.zeros((depth, depth), jnp.int32)
    for k in range(groups):
        residue = peer(member, k, paired)
        wanted = jnp.where(row // each == k, groups * (row - k * each) + residue, wanted)
    order = (wanted == column).astype(BF16)
    cache_copy.wait()
    sorted_rows = jnp.dot(order, held_cache[...], preferred_element_type=F32).astype(BF16)
    product = None
    for i, copy in enumerate(copies):
        copy.wait()
        at = slice(i * rows, (i + 1) * rows)
        part = jnp.dot(sorted_rows[:, at], held_weight[at], preferred_element_type=F32)
        product = part if product is None else product + part
    for k in range(groups):
        outs[k][...] = product[k * each : (k + 1) * each].astype(BF16)


def project(groups, paired, text_cache, w_kv):
    depth, features = text_cache.shape
    width = w_kv.shape[1]
    chunks = features // 128
    each = depth // groups
    return pl.pallas_call(
        functools.partial(project_kernel, groups, paired, chunks),
        in_specs=[HBM_SPEC, HBM_SPEC],
        out_specs=[VMEM_SPEC] * groups,
        out_shape=[jax.ShapeDtypeStruct((each, width), BF16)] * groups,
        scratch_shapes=[
            pltpu.VMEM((depth, features), BF16),
            pltpu.VMEM((features, width), BF16),
            pltpu.SemaphoreType.DMA,
            pltpu.SemaphoreType.DMA((chunks,)),
        ],
        compiler_params=kernel_params(),
        name="project",
    )(pltpu.with_memory_space_constraint(text_cache, pltpu.HBM), w_kv)


def select_kernel(groups, each, paired, dp_paired, n_texts, table, *refs):
    texts, pieces, outs, chip_text = refs[:n_texts], refs[n_texts : -2 * groups - 1], refs[-2 * groups - 1 : -1], refs[-1]
    depth = texts[0].shape[0]
    for i, text in enumerate(texts):
        chip_text[i * depth : (i + 1) * depth] = text[...]
    held = jnp.concatenate([piece[...] for piece in pieces], axis=0) if len(pieces) > 1 else pieces[0][...]
    total = held.shape[0]
    index, member = table[3, 0], table[3, 1]
    wanted_rows = groups * SAMPLES * each
    starts, firsts = [], []
    for k in range(groups):
        for s in range(SAMPLES):
            caption = peer(member, k, paired) * SAMPLES + s
            first = first_of_class(table[2, caption], member, groups)
            owner = table[1, caption]
            firsts.append(first)
            starts.append((owner ^ index if dp_paired else owner) * each + first)
    shape = (wanted_rows, total)
    target = spread_rows(starts, each, shape)
    inside = spread_rows(firsts, each, shape) < each
    chosen = ((target == lax.broadcasted_iota(jnp.int32, shape, 1)) & inside).astype(BF16)
    rows = jnp.dot(chosen, held, preferred_element_type=F32).astype(BF16)
    size, width = SAMPLES * each, rows.shape[1] // 2
    for k in range(groups):
        outs[k][...] = rows[k * size : (k + 1) * size, :width]
        outs[groups + k][...] = rows[k * size : (k + 1) * size, width:]


def select_rows(groups, each, paired, dp_paired, table, texts, pieces):
    width = pieces[0].shape[1]
    depth, features = texts[0].shape
    return pl.pallas_call(
        functools.partial(select_kernel, groups, each, paired, dp_paired, len(texts)),
        in_specs=[SMEM_SPEC] + [VMEM_SPEC] * (len(texts) + len(pieces)),
        out_specs=[VMEM_SPEC] * (2 * groups + 1),
        out_shape=[jax.ShapeDtypeStruct((SAMPLES * each, width // 2), BF16)] * (2 * groups)
        + [jax.ShapeDtypeStruct((len(texts) * depth, features), BF16)],
        compiler_params=kernel_params(),
        name="select_rows",
    )(table, *texts, *pieces)


LAST = (((1,), (1,)), ((), ()))
FIRST = (((0,), (0,)), ((), ()))


def value_grad_kernel(groups, each, paired, table, queries, cotangent, *refs):
    pieces, (probs, grad_values, scores, probs_rounded) = refs[:groups], refs[groups:]
    tokens, width = queries.shape
    slots = groups * SAMPLES * each
    heads = width // HEAD
    member = table[3, 1]
    split = table[3, 2]
    shape = (slots, tokens)
    rows = lax.broadcasted_iota(jnp.int32, shape, 0)
    position = jnp.zeros(shape, jnp.int32)
    length = jnp.zeros(shape, jnp.int32)
    sample = jnp.zeros(shape, jnp.int32)
    for c in range(groups):
        residue = peer(member, c, paired)
        for s in range(SAMPLES):
            caption = member * SAMPLES + s
            run = (c * SAMPLES + s) * each
            here = (rows >= run) & (rows < run + each)
            first = first_of_class(table[2, caption], residue, groups)
            position = jnp.where(here, groups * (first + rows - run) + residue - table[2, caption], position)
            length = jnp.where(here, table[0, caption], length)
            sample = jnp.where(here, s, sample)
    token_sample = (lax.broadcasted_iota(jnp.int32, shape, 1) >= split).astype(jnp.int32)
    allowed = (position < length) & (sample == token_sample)
    for h in range(heads):
        at = slice(h * HEAD, (h + 1) * HEAD)
        k = jnp.concatenate([piece[:, at] for piece in pieces], axis=0)
        scores[h] = lax.dot_general(k, queries[:, at], LAST, preferred_element_type=F32)
    for h in range(heads):
        masked = jnp.where(allowed, scores[h] * HEAD ** (-0.5), F32(-1e30))
        expon = jnp.exp(masked - jnp.max(masked, axis=0, keepdims=True))
        prob = expon / jnp.sum(expon, axis=0, keepdims=True)
        probs[h] = prob
        probs_rounded[h] = prob.astype(BF16)
    for h in range(heads):
        at = slice(h * HEAD, (h + 1) * HEAD)
        grad_values[:, at] = jnp.dot(probs_rounded[h], cotangent[:, at], preferred_element_type=F32).astype(BF16)


def value_grads(groups, each, paired, table, queries, grad_out, pieces):
    tokens, width = queries.shape
    slots = groups * SAMPLES * each
    heads = width // HEAD
    return pl.pallas_call(
        functools.partial(value_grad_kernel, groups, each, paired),
        in_specs=[SMEM_SPEC] + [VMEM_SPEC] * (2 + groups),
        out_specs=[VMEM_SPEC] * 2,
        out_shape=[
            jax.ShapeDtypeStruct((heads, slots, tokens), F32),
            jax.ShapeDtypeStruct((slots, width), BF16),
        ],
        scratch_shapes=[pltpu.VMEM((heads, slots, tokens), F32), pltpu.VMEM((heads, slots, tokens), BF16)],
        compiler_params=kernel_params(),
        name="value_gradients",
    )(table, queries, grad_out, *pieces)


def key_grad_kernel(groups, probs, queries, cotangent, grad_values, *refs):
    values, (score_grads, first_part, last_part, grad_both, prob_grads) = refs[:groups], refs[groups:]
    width = queries.shape[1]
    heads = width // HEAD
    scale = HEAD ** (-0.5)
    for h in range(heads):
        at = slice(h * HEAD, (h + 1) * HEAD)
        v = jnp.concatenate([piece[:, at] for piece in values], axis=0)
        prob_grads[h] = lax.dot_general(v, cotangent[:, at], LAST, preferred_element_type=F32)
    for h in range(heads):
        prob, prob_grad = probs[h], prob_grads[h]
        centre = jnp.sum(prob * prob_grad, axis=0, keepdims=True)
        score_grads[h] = (prob * (prob_grad - centre)).astype(BF16)
    for h in range(heads):
        at = slice(h * HEAD, (h + 1) * HEAD)
        grad_key = jnp.dot(score_grads[h], queries[:, at], preferred_element_type=F32) * scale
        grad_both[:, at] = grad_key.astype(BF16)
    grad_both[:, width:] = grad_values[...]
    cut = first_part.shape[1]
    first_part[...] = grad_both[:, :cut]
    last_part[...] = grad_both[:, cut:]


def key_grads(groups, probs, queries, grad_out, grad_values, values):
    tokens, width = queries.shape
    heads, slots, _ = probs.shape
    return pl.pallas_call(
        functools.partial(key_grad_kernel, groups),
        in_specs=[VMEM_SPEC] * (4 + groups),
        out_specs=[VMEM_SPEC] * 4,
        out_shape=[
            jax.ShapeDtypeStruct((heads, slots, tokens), BF16),
            jax.ShapeDtypeStruct((slots, FIRST_HEADS * HEAD), BF16),
            jax.ShapeDtypeStruct((slots, 2 * width - FIRST_HEADS * HEAD), BF16),
            jax.ShapeDtypeStruct((slots, 2 * width), BF16),
        ],
        scratch_shapes=[pltpu.VMEM((heads, slots, tokens), F32)],
        compiler_params=kernel_params(),
        name="key_gradients",
    )(probs, queries, grad_out, grad_values, *values)


def text_kernel(members, groups, each, depth, paired, dp_paired, table, text, score_grads, *refs):
    keys, (out, grad_query) = refs[:groups], refs[groups:]
    for h in range(score_grads.shape[0]):
        at = slice(h * HEAD, (h + 1) * HEAD)
        k = jnp.concatenate([piece[:, at] for piece in keys], axis=0)
        product = lax.dot_general(score_grads[h], k, FIRST, preferred_element_type=F32)
        grad_query[:, at] = (product * HEAD ** (-0.5)).astype(BF16)
    index, member = table[3, 0], table[3, 1]
    shape = (text.shape[0], out.shape[1])
    columns = lax.broadcasted_iota(jnp.int32, shape, 1)
    runs, place = columns // each, columns % each
    target = jnp.zeros(shape, jnp.int32)
    limit = jnp.zeros(shape, jnp.int32)
    run = 0
    for k in range(members):
        device = peer(member, k, paired)
        for c in range(groups):
            residue = peer(device, c, paired)
            for s in range(SAMPLES):
                caption = device * SAMPLES + s
                offset = table[2, caption]
                owner = table[1, caption]
                if dp_paired:
                    owner = owner - (owner & 1) + ((owner ^ index) & 1)
                base = owner * depth
                here = runs == run
                target = jnp.where(here, base + groups * first_of_class(offset, residue, groups) + residue, target)
                limit = jnp.where(here, base + offset + table[0, caption], limit)
                run += 1
    target = target + groups * place
    chosen = ((target == lax.broadcasted_iota(jnp.int32, shape, 0)) & (target < limit)).astype(BF16)
    out[...] = lax.dot_general(text[...], chosen, FIRST, preferred_element_type=F32).astype(BF16)


def slot_texts(members, groups, each, depth, paired, dp_paired, table, text, score_grads, keys):
    features = text.shape[1]
    return pl.pallas_call(
        functools.partial(text_kernel, members, groups, each, depth, paired, dp_paired),
        in_specs=[SMEM_SPEC] + [VMEM_SPEC] * (2 + groups),
        out_specs=[VMEM_SPEC] * 2,
        out_shape=[
            jax.ShapeDtypeStruct((features, members * groups * SAMPLES * each), BF16),
            jax.ShapeDtypeStruct((score_grads.shape[2], keys[0].shape[1]), BF16),
        ],
        compiler_params=kernel_params(),
        name="slot_texts",
    )(table, text, score_grads, *keys)


def weight_kernel(line, start, *refs):
    chosen_text, *grads = refs[:6] if line else refs[:2]
    out, every, built, sems = refs[-4:]
    at = slice(start, start + every.shape[1])
    if line:
        own, near, inner, second, outer = grads
        member = lax.axis_index("fsdp")
        is_inner = (member == 1) | (member == 2)
        each = own.shape[0]
        every[0:each] = own[:, at]
        every[each : 2 * each] = near[:, at]
        every[2 * each : 3 * each] = second[...]
        every[3 * each :] = jnp.where(is_inner, inner[:, at], outer[...])
    else:
        every[...] = grads[0][:, at]
    features = built.shape[0]
    sizes = [features // 16, 3 * features // 16] + [features // 4] * 3
    copies = []
    for i, rows in enumerate(sizes):
        begin = sum(sizes[:i])
        block = slice(begin, begin + rows)
        built[block] = jnp.dot(chosen_text[block], every[...], preferred_element_type=F32).astype(BF16)
        copy = pltpu.make_async_copy(
            built.at[pl.ds(begin, rows)],
            out.at[pl.ds(begin, rows), pl.ds(start, every.shape[1])],
            sems.at[i],
        )
        copy.start()
        copies.append(copy)
    for copy in copies:
        copy.wait()


def weight_grad(line, chosen_text, grads, start, size, before=None):
    features, slots = chosen_text.shape
    width = grads[0].shape[1]
    earlier = [] if before is None else [before]
    return pl.pallas_call(
        functools.partial(weight_kernel, line, start),
        in_specs=[VMEM_SPEC] * (1 + len(grads)) + [ANY_SPEC] * len(earlier),
        out_specs=ANY_SPEC,
        out_shape=jax.ShapeDtypeStruct((features, width), BF16),
        scratch_shapes=[
            pltpu.VMEM((slots, size), BF16),
            pltpu.VMEM((features, size), BF16),
            pltpu.SemaphoreType.DMA((5,)),
        ],
        input_output_aliases={1 + len(grads): 0} if earlier else {},
        compiler_params=kernel_params(),
        name="weight_gradient",
    )(chosen_text, *grads, *earlier)


def swap(x, axis, k):
    return lax.ppermute(x, axis, [(i, i ^ k) for i in range(lax.axis_size(axis))])


def gather_dp(x, paired):
    if not paired:
        return [lax.all_gather(x, "dp", axis=0, tiled=True)]
    near = {0: x}
    for k in range(2, lax.axis_size("dp"), 2):
        near[k] = swap(x, "dp", k)
    for k in list(near):
        near[k + 1] = swap(near[k], "dp", 1)
    return [near[k] for k in sorted(near)]


def gather_chips(x):
    size = lax.axis_size("dp")
    cores = [list(range(core, size, 2)) for core in range(2)]
    return lax.all_gather(x, "dp", axis=0, tiled=True, axis_index_groups=cores)


def reduce_line(pieces, members, paired):
    if paired:
        distances = sorted(range(1, members), key=lambda k: (k != 2, k))
        return [pieces[0]] + [swap(pieces[k], "fsdp", k) for k in distances]
    return exchange(pieces, paired)


def exchange(pieces, paired):
    if paired:
        return [pieces[0]] + [swap(pieces[k], "fsdp", k) for k in range(1, len(pieces))]
    came = lax.all_to_all(jnp.stack(pieces), "fsdp", 0, 0, tiled=True)
    return [came[k] for k in range(len(pieces))]


def gather_line(parts, both, beside):
    near_pairs = [(0, 1), (1, 0), (2, 3), (3, 2)]
    middle_pairs = [(1, 2), (2, 1)]
    outward = [(1, 0), (2, 3)]
    second = [swap(part, "fsdp", 2) for part in parts]
    near = lax.ppermute(both, "fsdp", near_pairs)
    second[1], beside = lax.optimization_barrier((second[1], beside))
    outer = [lax.ppermute(piece, "fsdp", outward) for piece in second]
    late, _ = lax.optimization_barrier((both, second[1]))
    inner = lax.ppermute(late, "fsdp", middle_pairs)
    return near, inner, second, outer, beside


def shards(
    queries, grad_out, text_cache, w_kv, image_counts, caption_lens, caption_owner, caption_offset
):
    members = lax.axis_size("fsdp")
    line = members == 4
    groups = members
    paired = line
    dp_paired = power_of_two(lax.axis_size("dp")) and lax.axis_size("dp") <= 8
    depth = text_cache.shape[0]
    each = depth // groups
    width = queries.shape[1]

    partials = project(groups, paired, text_cache, w_kv)
    partials, late_cache = lax.optimization_barrier((partials, text_cache))
    texts = [late_cache, swap(late_cache, "dp", 1)] if dp_paired else [late_cache]
    came = reduce_line(partials, members, paired)
    table = scalar_table(image_counts, caption_lens, caption_owner, caption_offset)
    rows = sum(piece.astype(F32) for piece in came).astype(BF16)
    class_rows = gather_dp(rows, dp_paired)
    *outgoing, chip_text = select_rows(groups, each, paired, dp_paired, table, texts, class_rows)
    keys = exchange(outgoing[:groups], paired)
    values = exchange(outgoing[groups:], paired)
    probs, grad_values = value_grads(groups, each, paired, table, queries, grad_out, keys)
    grad_values, probs = lax.optimization_barrier((grad_values, probs))
    score_grads, *parts, grad_both = key_grads(groups, probs, queries, grad_out, grad_values, values)
    parts, grad_both, chip_text = lax.optimization_barrier((parts, grad_both, chip_text))
    if dp_paired:
        text = gather_chips(chip_text)
    else:
        text = lax.all_gather(chip_text, "dp", axis=0, tiled=True)
    if line:
        near, inner, second, outer, text = gather_line(parts, grad_both, text)
        operands = [[grad_both, near, inner, second[i], outer[i]] for i in range(2)]
    else:
        operands = [[lax.all_gather(grad_both, "fsdp", axis=0, tiled=True)]] * 2
    chosen_text, grad_query = slot_texts(members, groups, each, depth, paired, dp_paired, table, text, score_grads, keys)
    cut = parts[0].shape[1]
    grad_weight = weight_grad(line, chosen_text, operands[0], 0, cut)
    grad_weight = weight_grad(line, chosen_text, operands[1], cut, 2 * width - cut, grad_weight)
    return grad_query, grad_weight[None]


def solution(mesh):
    in_specs = (
        P(("dp", "fsdp"), None),
        P(("dp", "fsdp"), None),
        P("dp", "fsdp"),
        P("fsdp", None),
        P(("dp", "fsdp"), None),
        P("dp", None),
        P("dp", None),
        P("dp", None),
    )
    out_specs = (P(("dp", "fsdp"), None), P("dp", "fsdp", None))
    return jax.shard_map(shards, mesh=mesh, in_specs=in_specs, out_specs=out_specs, check_vma=False)
```
